32 devices in a mesh: real: 2 (over y), slab: 4 (over z), pencil: 2 (over x), sub: 2 (over core).
Axes of the slice: x: 2, y: 2, z: 4, core: 2. Of those that a mesh axis runs over, the one named last changes fastest.
Arguments:
- permeability: float32 [128, 64, 256], P(('real', 'slab'), ('pencil', 'sub')), parts along dimension 0, may hold values from 0.1 to 10
- source: float32 [128, 64, 256], P(('real', 'slab'), ('pencil', 'sub')), parts along dimension 0, may hold values from -24 to 24
- pressure: float32 [128, 64, 256], P(('real', 'slab'), ('pencil', 'sub')), parts along dimension 0, may hold values from -24 to 24
- aggregate: int32 [128], P('real'), parts along dimension 0, may hold values from 0 to 31, as said below
Outputs:
- pressure_out: float32 [128, 64, 256], P(('real', 'slab'), ('pencil', 'sub')), parts along dimension 0
The draws below stay inside these ranges and needn't reach their ends.
There are 2 independent parts, one for each index of `real`. The reference program is written for one: setup_inputs(seed, part) draws one part's arguments, and reference() takes and returns one part's arrays. A program takes and returns all parts, laid end to end along the dimension named above; each array names one. Nothing has to cross between parts.
Inputs may be any that keep to these rules, and one draw needn't show every extreme that they name: `aggregate`: never falls along its dimension; each value covers 1 to 4 consecutive positions, some value exactly 4; positions k * 16 - 1 and k * 16 always hold the same value.
All inputs are finite; a program needn't handle non-finite values.
Results may differ from the reference program's by a relative error of at most 0.000068.
Values sent between devices are 32-bit elements; how exact they have to be, the bound alone decides.
A program may use at most 64 MiB of HBM per device.

```python
import math
import jax
import jax.numpy as jnp

NZ = 256
NU = 2
NCS = 4
NX = 64
NY = 64
NXC = 32


def draw_aggregate(key, part):
    patterns = jnp.array([[2, 2, 2, 2], [1, 1, 2, 4], [4, 1, 1, 2], [1, 4, 1, 2], [3, 1, 1, 3], [1, 3, 2, 2], [2, 1, 1, 4]], dtype=jnp.int32)
    block_count = NX // 8 - 1
    picks = jax.random.randint(jax.random.fold_in(key, 11), (block_count,), 0, 7)
    picks = jnp.concatenate([jnp.ones((1,), jnp.int32), picks[1:]])
    block_lens = patterns[picks].reshape(-1)
    lengths = jnp.concatenate([jnp.ones((1,), jnp.int32), block_lens, jnp.array([2, 2, 3], dtype=jnp.int32)])
    ends = jnp.cumsum(lengths).astype(jnp.int32)
    positions = jnp.arange(NX, dtype=jnp.int32)
    return jnp.sum((ends[None, :] <= positions[:, None]).astype(jnp.int32), axis=1).astype(jnp.int32)


def block_scale(own_key, shape, split, smallest, top_value):
    factor_of, own = 1.0, jax.random.fold_in(own_key, 6)
    for dim, parts in split:
        steps = jnp.exp(jax.random.uniform(jax.random.fold_in(own, dim), (parts,), jnp.float32, smallest / len(split), top_value / len(split)))
        factor_of = factor_of * jnp.repeat(steps, shape[dim] // parts).reshape([-1 if axis == dim else 1 for axis in range(len(shape))])
    return factor_of


def normal_values(key, shape, scale, reach, shards=(), kind=jnp.bfloat16):
    values = jax.random.normal(key, shape, jnp.float32) * scale
    if len(shards) > 0:
        values = block_scale(key, shape, shards, -0.22, 0.18) * values
    return jnp.clip(values, min=-reach, max=reach).astype(kind)


def setup_inputs(seed: int = 0, part: int = 0) -> dict:
    keys = jax.random.split(jax.random.key(seed), 5)
    part_keys = jax.random.split(jax.random.fold_in(keys[4], part), 5)
    return {
        "permeability": jnp.clip(jnp.exp(math.log(10.0) - 4.6051702 * jax.random.uniform(part_keys[0], (NX, NY, NZ), jnp.float32) ** block_scale(part_keys[0], (NX, NY, NZ), ((0, 4), (1, 4)), -0.2, 0.2)), 0.1, 10.0),
        "source": normal_values(part_keys[1], (NX, NY, NZ), 4.0, 24.0, ((0, 4), (1, 4)), jnp.float32),
        "pressure": normal_values(part_keys[2], (NX, NY, NZ), 4.0, 24.0, ((0, 4), (1, 4)), jnp.float32),
        "aggregate": draw_aggregate(jax.random.fold_in(jax.random.fold_in(keys[4], part), 71), part),
    }


OMEGA = 0.8


def harmonic(lower_k, upper_k):
    return 2.0 * lower_k * upper_k / (lower_k + upper_k)


def geometry(permeability):
    count_x, count_y, count_z = permeability.shape
    kind = permeability.dtype
    face_x = harmonic(permeability[:-1], permeability[1:])
    face_y = harmonic(permeability[:, :-1], permeability[:, 1:])
    face_z = harmonic(permeability[:, :, :-1], permeability[:, :, 1:])
    zero_x = jnp.zeros_like(permeability[:1])
    zero_y = jnp.zeros_like(permeability[:, :1])
    zero_z = jnp.zeros_like(permeability[:, :, :1])
    face_west = jnp.concatenate([zero_x, face_x], axis=0)
    face_east = jnp.concatenate([face_x, zero_x], axis=0)
    face_south = jnp.concatenate([zero_y, face_y], axis=1)
    face_north = jnp.concatenate([face_y, zero_y], axis=1)
    face_below = jnp.concatenate([zero_z, face_z], axis=2)
    face_above = jnp.concatenate([face_z, zero_z], axis=2)
    index_x = jnp.arange(count_x)
    index_y = jnp.arange(count_y)
    index_z = jnp.arange(count_z)
    ends_x = (index_x == 0).astype(kind) + (index_x == count_x - 1).astype(kind)
    ends_y = (index_y == 0).astype(kind) + (index_y == count_y - 1).astype(kind)
    ends_z = (index_z == 0).astype(kind) + (index_z == count_z - 1).astype(kind)
    edges = ends_x[:, None, None] + ends_y[None, :, None] + ends_z[None, None, :]
    boundary = 2.0 * permeability * edges
    diagonal = face_west + face_east + face_south + face_north + face_below + face_above + boundary
    return face_west, face_east, face_south, face_north, face_below, face_above, boundary, diagonal


def apply_fine(field_in, faces_all):
    face_west, face_east, face_south, face_north, face_below, face_above, boundary, diagonal = faces_all
    padded = jnp.pad(field_in, 1)
    center = padded[1:-1, 1:-1, 1:-1]
    beside_all = face_west * padded[:-2, 1:-1, 1:-1] + face_east * padded[2:, 1:-1, 1:-1]
    beside_all = beside_all + face_south * padded[1:-1, :-2, 1:-1] + face_north * padded[1:-1, 2:, 1:-1]
    beside_all = beside_all + face_below * padded[1:-1, 1:-1, :-2] + face_above * padded[1:-1, 1:-1, 2:]
    return diagonal * center - beside_all


def reference(permeability, source, pressure, aggregate):
    faces_all = geometry(permeability)
    face_east = faces_all[1]
    face_north = faces_all[3]
    face_above = faces_all[5]
    boundary = faces_all[6]
    diagonal = faces_all[7]
    count_x, count_y, count_z = permeability.shape
    half_y = count_y // 2
    half_z = count_z // 2
    for sweep_index in range(NU):
        pressure = pressure + OMEGA * (source - apply_fine(pressure, faces_all)) / diagonal
    residual = source - apply_fine(pressure, faces_all)

    def pair_sum(block):
        return block.reshape(count_x, half_y, 2, half_z, 2).sum(axis=(2, 4))

    def by_plane(block):
        return jax.ops.segment_sum(block, aggregate, num_segments=NXC)

    crossing = jnp.concatenate([aggregate[:-1] != aggregate[1:], jnp.zeros((1,), dtype=bool)]).astype(permeability.dtype)
    coarse_rhs = by_plane(pair_sum(residual))
    coarse_east = by_plane(pair_sum(face_east * crossing[:, None, None]))
    coarse_north = by_plane(face_north[:, 1::2].reshape(count_x, half_y, half_z, 2).sum(axis=3))
    coarse_above = by_plane(face_above[:, :, 1::2].reshape(count_x, half_y, 2, half_z).sum(axis=2))
    coarse_bound = by_plane(pair_sum(boundary))
    coarse_west = jnp.concatenate([jnp.zeros_like(coarse_east[:1]), coarse_east[:-1]], axis=0)
    coarse_south = jnp.concatenate([jnp.zeros_like(coarse_north[:, :1]), coarse_north[:, :-1]], axis=1)
    coarse_below = jnp.concatenate([jnp.zeros_like(coarse_above[:, :, :1]), coarse_above[:, :, :-1]], axis=2)
    coarse_diag = coarse_east + coarse_west + coarse_north + coarse_south + coarse_above + coarse_below + coarse_bound
    correction = jnp.zeros_like(coarse_rhs)
    for sweep_index in range(NCS):
        padded = jnp.pad(correction, 1)
        center = padded[1:-1, 1:-1, 1:-1]
        beside_all = coarse_east * padded[2:, 1:-1, 1:-1] + coarse_west * padded[:-2, 1:-1, 1:-1]
        beside_all = beside_all + coarse_north * padded[1:-1, 2:, 1:-1] + coarse_south * padded[1:-1, :-2, 1:-1]
        beside_all = beside_all + coarse_above * padded[1:-1, 1:-1, 2:] + coarse_below * padded[1:-1, 1:-1, :-2]
        correction = center + OMEGA * (coarse_rhs - (coarse_diag * center - beside_all)) / coarse_diag
    spread = jnp.take(correction, aggregate, axis=0)
    spread = jnp.repeat(jnp.repeat(spread, 2, axis=1), 2, axis=2)
    pressure = pressure + spread
    for sweep_index in range(NU):
        pressure = pressure + OMEGA * (source - apply_fine(pressure, faces_all)) / diagonal
    return pressure
```

```python
import functools
import jax
import jax.numpy as jnp
from jax import lax
from jax.experimental import pallas as pl
from jax.experimental.pallas import tpu as pltpu
from jax.sharding import PartitionSpec as P

OMEGA = 0.8
MESH = pl.DeviceIdType.MESH
HIGH = lax.Precision.HIGHEST

DIRS = [(dx, dy) for dx in (1, 0, -1) for dy in (1, 0, -1) if (dx, dy) != (0, 0)]
FROM = {0: 0, 1: 1, -1: 2}


def dot(a, b):
    return jnp.dot(a, b, precision=HIGH, preferred_element_type=jnp.float32)


def kernel(
    agg, k_in, s_in, p_in, out,
    ke, se, pe, khalo, shalo, phalo, fx, fy, fz, dg, wt, p1, p2, rr, rhalo,
    fields, cm, cl, cr, cs, ext, corr, local_sem, send_sem, recv_sem,
):
    f32 = jnp.float32
    width = 16
    slab, slabs = lax.axis_index("slab"), lax.axis_size("slab")
    subs = lax.axis_size("sub")
    rows = lax.axis_size("pencil") * subs
    row = lax.axis_index("pencil") * subs + lax.axis_index("sub")

    loads = [
        pltpu.make_async_copy(src, dst.at[3:19, 0:16], local_sem.at[i])
        for i, (src, dst) in enumerate(((k_in, ke), (p_in, pe), (s_in, se)))
    ]
    for load in loads:
        load.start()

    def exists(dx, dy):
        ok = None
        for pos, step, count in ((slab, dx, slabs), (row, dy, rows)):
            if step:
                here = (pos + step < count) if step > 0 else (pos > 0)
                ok = here if ok is None else jnp.logical_and(ok, here)
        return ok

    def device(dx, dy):
        r = row + dy
        return {"slab": slab + dx, "pencil": r // subs, "sub": r % subs}

    barrier = pltpu.get_barrier_semaphore()
    for dx, dy in DIRS:
        @pl.when(exists(dx, dy))
        def _():
            pl.semaphore_signal(barrier, inc=1, device_id=device(dx, dy), device_id_type=MESH)
    near_x = 1 + (slab > 0).astype(jnp.int32) + (slab < slabs - 1).astype(jnp.int32)
    near_y = 1 + (row > 0).astype(jnp.int32) + (row < rows - 1).astype(jnp.int32)

    def message(kind, d, src, dst):
        return pltpu.make_async_remote_copy(
            src_ref=src, dst_ref=dst,
            send_sem=send_sem.at[kind * 8 + d], recv_sem=recv_sem.at[kind * 8 + d],
            device_id=device(*DIRS[d]), device_id_type=MESH,
        )

    def fine_message(kind, d, body, halo, wide, corner):
        dx, dy = DIRS[d]
        if dy == 0:
            src0 = 19 - wide if dx > 0 else 3
            dst0 = 3 - wide if dx > 0 else 19
            return message(kind, d, body.at[src0:src0 + wide, 0:16], body.at[dst0:dst0 + wide, 0:16])
        src_row = 8 if dy > 0 else 0
        if dx == 0:
            src0, dst0, length = 3, 3, 16
        else:
            src0 = 19 - corner if dx > 0 else 3
            dst0 = 3 - corner if dx > 0 else 19
            length = corner
        return message(
            kind, d, body.at[src0:src0 + length, src_row:src_row + 8],
            halo.at[FROM[dy] - 1, dst0:dst0 + length],
        )

    def coarse_message(kind, d, q0, q1):
        dx, dy = DIRS[d]
        here = FROM[dy]
        qs = pl.ds(q0, q1 - q0)
        if dx > 0:
            return message(kind, d, cs.at[qs], cl.at[here, qs])
        if dx < 0:
            return message(kind, d, cm.at[0, qs, 0:32], cr.at[here, qs])
        return message(kind, d, cm.at[0, qs], cm.at[here, qs])

    kinds = {
        "k": lambda d: fine_message(0, d, ke, khalo, 3, 2),
        "p": lambda d: fine_message(1, d, pe, phalo, 3, 2),
        "s": lambda d: fine_message(2, d, se, shalo, 2, 1),
        "coef": lambda d: coarse_message(3, d, 1, 5),
        "rhs": lambda d: coarse_message(4, d, 0, 1),
        "post": lambda d: fine_message(5, d, rr, rhalo, 1, 0),
    }

    def each(name):
        return [d for d in range(8) if name != "post" or 0 in DIRS[d]]

    def send(name):
        for d in each(name):
            @pl.when(exists(*DIRS[d]))
            def _():
                kinds[name](d).start()

    def receive(name):
        for d in each(name):
            dx, dy = DIRS[d]
            @pl.when(exists(-dx, -dy))
            def _():
                kinds[name](d).wait_recv()

    def sent(name):
        for d in each(name):
            @pl.when(exists(*DIRS[d]))
            def _():
                kinds[name](d).wait_send()

    for load in loads:
        load.wait()
    pl.semaphore_wait(barrier, near_x * near_y - 1)
    send("k")
    send("p")
    send("s")

    def clear(ref, *index):
        view = ref.at[index]
        view[...] = jnp.zeros(view.shape, f32)

    for ref, halo, wide, corner in ((ke, khalo, 3, 2), (pe, phalo, 3, 2), (se, shalo, 2, 1)):
        for at in (slice(0, 3 - corner), slice(19 + corner, 22)):
            clear(halo, slice(0, 2), at)
        if wide < 3:
            clear(ref, slice(0, 1))
            clear(ref, slice(21, 22))
    for dx, dy in DIRS:
        @pl.when(jnp.logical_not(exists(-dx, -dy)))
        def _():
            for ref, halo, wide, corner in (
                (ke, khalo, 3, 2), (pe, phalo, 3, 2), (se, shalo, 2, 1), (rr, rhalo, 1, 0),
            ):
                if dy == 0:
                    at = slice(3 - wide, 3) if dx > 0 else slice(19, 19 + wide)
                    clear(ref, at, slice(0, 16))
                else:
                    lo, hi = {0: (3, 19), 1: (3 - corner, 3), -1: (19, 19 + corner)}[dx]
                    if hi > lo:
                        clear(halo, FROM[dy] - 1, slice(lo, hi))
            part = {0: cm, 1: cl, -1: cr}[dx]
            clear(part, FROM[dy])

    low_half = lax.broadcasted_iota(jnp.int32, (8, 256), 0) < 4
    y_at = lax.broadcasted_iota(jnp.int32, (24, 256), 0)
    z_at = lax.broadcasted_iota(jnp.int32, (24, 256), 1)
    y_rel = jnp.where(y_at < 20, y_at, y_at - 24)
    y_glob = y_rel + row * width
    ends_yz = (
        (y_glob == 0).astype(f32) + (y_glob == rows * width - 1).astype(f32)
        + (z_at == 0).astype(f32) + (z_at == 255).astype(f32)
    )
    odd_y = (y_at & 1) == 1
    odd_z = (z_at & 1) == 1

    def loop(lo, hi, step, unroll=2):
        def run(i, carry):
            step(i)
            return carry
        lax.fori_loop(lo, hi, run, 0, unroll=unroll)

    def set_rim(body, halo, lo, hi):
        def step(i):
            body[i, 16:24] = jnp.where(low_half, halo[1, i], halo[0, i])
        loop(lo, hi, step)

    def next_y(v):
        return pltpu.roll(v, 23, 0)

    def prev_y(v):
        return pltpu.roll(v, 1, 0)

    def next_z(v):
        return pltpu.roll(v, 255, 1)

    def prev_z(v):
        return pltpu.roll(v, 1, 1)

    def face(a, b):
        total = a + b
        return 2.0 * a * b / jnp.where(total > 0, total, 1.0)

    ids = [agg[slab * width + x] for x in range(width)]
    slots = [i - ids[0] for i in ids]
    live = slots[15]
    col = lax.broadcasted_iota(jnp.int32, (1, 256), 1)
    slot_col = jnp.zeros((1, 256), jnp.int32)
    cross_col = jnp.zeros((1, 256), jnp.int32)
    for x in range(width):
        inside = (col >> 4) == x
        slot_col = jnp.where(inside, slots[x], slot_col)
        if x < 15:
            cross_col = jnp.where(inside, (ids[x] != ids[x + 1]).astype(jnp.int32), cross_col)
    r168 = lax.broadcasted_iota(jnp.int32, (168, 256), 0)
    c168 = lax.broadcasted_iota(jnp.int32, (168, 256), 1)
    want = jnp.where(r168 < 128, r168 >> 3, (r168 >> 3) - 20 + live)
    gather = ((want == slot_col) & ((r168 & 7) == ((c168 & 15) >> 1))).astype(f32)
    gather_east = gather * cross_col.astype(f32)
    zr = lax.broadcasted_iota(jnp.int32, (256, 128), 0)
    zc = lax.broadcasted_iota(jnp.int32, (256, 128), 1)
    pair_z = ((zr >> 1) == zc).astype(f32)

    def coarsen(q, field, how):
        sums = dot(dot(how, field), pair_z)
        cm[0, q] = sums[0:128]
        cs[q] = sums[128:168]

    receive("k")
    set_rim(ke, khalo, 0, 22)

    def x_faces(i):
        fx[i] = face(ke[i], ke[i + 1])
    loop(0, 21, x_faces)

    def other_faces(i):
        k = ke[i]
        north = face(k, next_y(k))
        above = jnp.where(z_at == 255, 0.0, face(k, next_z(k)))
        south, below = prev_y(north), prev_z(above)
        x_glob = slab * width + i - 3
        ends_x = (x_glob == 0).astype(f32) + (x_glob == slabs * width - 1).astype(f32)
        bound = 2.0 * k * (ends_yz + ends_x)
        fy[i] = north
        fz[i] = above
        diag = fx[i - 1] + fx[i] + north + south + above + below + bound
        dg[i] = diag
        wt[i] = OMEGA / jnp.where(diag > 0, diag, 1.0)
        return north, above, south, below, bound

    def plain_faces(i):
        other_faces(i)

    def own_faces(i):
        north, above, south, below, bound = other_faces(i)
        fields[1, i - 3] = fx[i, 0:16]
        fields[2, i - 3] = jnp.where(odd_y, north, 0.0)[0:16]
        fields[3, i - 3] = jnp.where(odd_z, above, 0.0)[0:16]
        whole = bound + jnp.where(odd_y, north, south) + jnp.where(odd_z, above, below)
        fields[4, i - 3] = whole[0:16]

    loop(3, 19, own_faces)
    for q in range(1, 5):
        coarsen(q, fields[q].reshape(256, 256), gather_east if q == 1 else gather)
    send("coef")
    loop(1, 3, plain_faces)
    loop(19, 21, plain_faces)

    def beside(src, i):
        v = src[i]
        north, above = fy[i], fz[i]
        around = fx[i - 1] * src[i - 1] + fx[i] * src[i + 1]
        around = around + (north * next_y(v) + prev_y(north * v))
        return v, around + (above * next_z(v) + prev_z(above * v))

    def sweep(src, dst, lo, hi):
        def step(i):
            v, around = beside(src, i)
            dst[i] = (1.0 - OMEGA) * v + wt[i] * (se[i] + around)
        loop(lo, hi, step)

    receive("p")
    set_rim(pe, phalo, 0, 22)
    receive("s")
    set_rim(se, shalo, 1, 21)
    sweep(pe, p1, 1, 21)
    sweep(p1, p2, 2, 20)

    def residual(i):
        v, around = beside(p2, i)
        fields[0, i - 3] = (se[i] - dg[i] * v + around)[0:16]
    loop(3, 19, residual)
    coarsen(0, fields[0].reshape(256, 256), gather)
    send("rhs")

    rp = lax.broadcasted_iota(jnp.int32, (384, 64), 0)
    cp = lax.broadcasted_iota(jnp.int32, (384, 64), 1)
    place = (((rp >> 4) - (cp >> 4) == 4 + live) & ((rp & 15) == (cp & 15))).astype(f32)
    low_coarse = lax.broadcasted_iota(jnp.int32, (1, 8, 128), 1) < 4

    def joined(part, q, count):
        own = part[0, q].reshape(count, 8, 128)
        below = part[1, q].reshape(count, 8, 128)
        above = part[2, q].reshape(count, 8, 128)
        return jnp.concatenate([own, jnp.where(low_coarse, above, below)], axis=1)

    def extend(q):
        after = dot(place, joined(cr, q, 4).reshape(64, 128)).reshape(24, 16, 128)
        ext[q] = after
        ext[q, 0:5] += joined(cl, q, 5)
        ext[q, 4:20] += joined(cm, q, 16)

    receive("coef")
    for q in range(1, 5):
        extend(q)
    zl = lax.broadcasted_iota(jnp.int32, (16, 128), 1)
    def diagonal(t):
        diag = ext[4, t] + ext[1, t] + ext[1, t - 1]
        corr[2, t] = OMEGA / jnp.where(diag > 0, diag, 1.0)
    loop(1, 23, diagonal)
    receive("rhs")
    extend(0)

    def first(t):
        corr[0, t] = corr[2, t] * ext[0, t]
    loop(1, 23, first)
    for number, (lo, hi) in enumerate(((2, 22), (3, 21), (4, 20))):
        src, dst = number % 2, (number + 1) % 2
        def coarse_sweep(t):
            v = corr[src, t]
            north, above = ext[2, t], ext[3, t]
            around = ext[1, t] * corr[src, t + 1] + ext[1, t - 1] * corr[src, t - 1]
            around = around + (north * pltpu.roll(v, 15, 0) + pltpu.roll(north * v, 1, 0))
            around = around + (above * pltpu.roll(v, 127, 1) + pltpu.roll(above * v, 1, 1))
            corr[dst, t] = (1.0 - OMEGA) * v + corr[2, t] * (ext[0, t] + around)
        loop(lo, hi, coarse_sweep)

    ru = lax.broadcasted_iota(jnp.int32, (24, 256), 0)
    cu = lax.broadcasted_iota(jnp.int32, (24, 256), 1)
    same_y = (cu & 15) == jnp.where(ru < 20, ru >> 1, (ru >> 1) + 4)
    spread = jnp.concatenate(
        [(same_y & ((cu >> 4) == slots[x])).astype(f32) for x in range(width)], axis=0
    )
    er = lax.broadcasted_iota(jnp.int32, (128, 256), 0)
    ec = lax.broadcasted_iota(jnp.int32, (128, 256), 1)
    twice_z = ((ec >> 1) == er).astype(f32)
    fine = dot(dot(spread, corr[1, 4:20].reshape(256, 128)), twice_z).reshape(16, 24, 256)
    p1[3:19] = p2[3:19] + fine
    p1[2] = p2[2] + fine[0]
    p1[19] = p2[19] + fine[15]
    sweep(p1, rr, 3, 19)
    send("post")
    receive("post")
    set_rim(rr, rhalo, 3, 19)

    def last(i):
        v, around = beside(rr, i)
        out[i - 3] = ((1.0 - OMEGA) * v + wt[i] * (se[i] + around))[0:16]
    loop(3, 19, last)
    for name in kinds:
        sent(name)


def body(permeability, source, pressure, aggregate):
    f32 = jnp.float32
    shape = permeability.shape
    block = pltpu.VMEM((22, 24, 256), f32)
    halo = pltpu.VMEM((2, 22, 8, 256), f32)
    hbm = pl.BlockSpec(memory_space=pl.ANY)
    return pl.pallas_call(
        kernel,
        out_shape=jax.ShapeDtypeStruct(shape, f32),
        in_specs=[pl.BlockSpec(memory_space=pltpu.SMEM), hbm, hbm, hbm],
        out_specs=pl.BlockSpec(memory_space=pltpu.VMEM),
        scratch_shapes=[block, block, block, halo, halo, halo]
        + [block] * 8
        + [
            halo,
            pltpu.VMEM((5, 16, 16, 256), f32),
            pltpu.VMEM((3, 5, 128, 128), f32),
            pltpu.VMEM((3, 5, 40, 128), f32),
            pltpu.VMEM((3, 5, 32, 128), f32),
            pltpu.VMEM((5, 40, 128), f32),
            pltpu.VMEM((5, 24, 16, 128), f32),
            pltpu.VMEM((3, 24, 16, 128), f32),
            pltpu.SemaphoreType.DMA((3,)),
            pltpu.SemaphoreType.DMA((48,)),
            pltpu.SemaphoreType.DMA((48,)),
        ],
        compiler_params=pltpu.CompilerParams(
            collective_id=0, has_side_effects=True, vmem_limit_bytes=40 * 2**20
        ),
    )(aggregate, permeability, source, pressure)


def solution(mesh):
    spec = P(("real", "slab"), ("pencil", "sub"), None)
    return jax.shard_map(
        body, mesh=mesh, in_specs=(spec, spec, spec, P("real")), out_specs=spec, check_vma=False
    )
```

```python
import functools
import jax
import jax.numpy as jnp
from jax import lax
from jax.experimental import pallas as pl
from jax.experimental.pallas import tpu as pltpu
from jax.sharding import PartitionSpec as P

OMEGA = 0.8
MESH = pl.DeviceIdType.MESH

DIRS = [(dx, dy) for dx in (1, 0, -1) for dy in (1, 0, -1) if (dx, dy) != (0, 0)]
FROM = {0: 0, 1: 1, -1: 2}


def dot(a, b):
    return jnp.dot(a, b, preferred_element_type=jnp.float32)


def halves(v):
    upper = v.astype(jnp.bfloat16)
    return upper, (v - upper.astype(jnp.float32)).astype(jnp.bfloat16)


def kernel(
    agg, k_in, s_in, p_in, out,
    ke, se, pe, khalo, shalo, phalo, fx, fy, fz, dg, wt, p1, p2, rr, rhalo,
    edge, result, fields, cm, cl, cr, cs, ext, corr, local_sem, send_sem, recv_sem,
):
    f32 = jnp.float32
    width = 16
    slab, slabs = lax.axis_index("slab"), lax.axis_size("slab")
    subs = lax.axis_size("sub")
    rows = lax.axis_size("pencil") * subs
    row = lax.axis_index("pencil") * subs + lax.axis_index("sub")

    loads = [
        pltpu.make_async_copy(src, dst.at[3:19, 0:16], local_sem.at[i])
        for i, (src, dst) in enumerate(((k_in, ke), (p_in, pe), (s_in, se)))
    ]
    for load in loads:
        load.start()

    def exists(dx, dy):
        ok = None
        for pos, step, count in ((slab, dx, slabs), (row, dy, rows)):
            if step:
                here = (pos + step < count) if step > 0 else (pos > 0)
                ok = here if ok is None else jnp.logical_and(ok, here)
        return ok

    def device(dx, dy):
        r = row + dy
        return {"slab": slab + dx, "pencil": r // subs, "sub": r % subs}

    barrier = pltpu.get_barrier_semaphore()
    for dx, dy in DIRS:
        @pl.when(exists(dx, dy))
        def _():
            pl.semaphore_signal(barrier, inc=1, device_id=device(dx, dy), device_id_type=MESH)
    near_x = 1 + (slab > 0).astype(jnp.int32) + (slab < slabs - 1).astype(jnp.int32)
    near_y = 1 + (row > 0).astype(jnp.int32) + (row < rows - 1).astype(jnp.int32)

    def message(kind, d, src, dst):
        return pltpu.make_async_remote_copy(
            src_ref=src, dst_ref=dst,
            send_sem=send_sem.at[kind * 8 + d], recv_sem=recv_sem.at[kind * 8 + d],
            device_id=device(*DIRS[d]), device_id_type=MESH,
        )

    def fine_message(kind, d, body, halo, wide, corner):
        dx, dy = DIRS[d]
        if dy == 0:
            src0 = 19 - wide if dx > 0 else 3
            dst0 = 3 - wide if dx > 0 else 19
            return message(kind, d, body.at[src0:src0 + wide, 0:16], body.at[dst0:dst0 + wide, 0:16])
        src_row = 8 if dy > 0 else 0
        if dx == 0:
            src0, dst0, length = 3, 3, 16
        else:
            src0 = 19 - corner if dx > 0 else 3
            dst0 = 3 - corner if dx > 0 else 19
            length = corner
        return message(
            kind, d, body.at[src0:src0 + length, src_row:src_row + 8],
            halo.at[FROM[dy] - 1, dst0:dst0 + length],
        )

    def coarse_message(kind, d, q0, q1):
        dx, dy = DIRS[d]
        here = FROM[dy]
        qs = pl.ds(q0, q1 - q0)
        if dx > 0:
            return message(kind, d, cs.at[qs], cl.at[here, qs])
        if dx < 0:
            return message(kind, d, cm.at[0, qs, 0:32], cr.at[here, qs])
        return message(kind, d, cm.at[0, qs], cm.at[here, qs])

    def post_message(d):
        dx, dy = DIRS[d]
        if dy == 0:
            return fine_message(5, d, rr, None, 1, 0)
        return message(5, d, edge.at[FROM[dy] - 1], rhalo.at[FROM[dy] - 1])

    kinds = {
        "k": lambda d: fine_message(0, d, ke, khalo, 3, 2),
        "p": lambda d: fine_message(1, d, pe, phalo, 3, 2),
        "s": lambda d: fine_message(2, d, se, shalo, 2, 1),
        "coef": lambda d: coarse_message(3, d, 1, 5),
        "rhs": lambda d: coarse_message(4, d, 0, 1),
        "post": post_message,
    }

    def each(name):
        return [d for d in range(8) if name != "post" or 0 in DIRS[d]]

    def send(name):
        for d in each(name):
            @pl.when(exists(*DIRS[d]))
            def _():
                kinds[name](d).start()

    def receive(name):
        for d in each(name):
            dx, dy = DIRS[d]
            @pl.when(exists(-dx, -dy))
            def _():
                kinds[name](d).wait_recv()

    def sent(name):
        for d in each(name):
            @pl.when(exists(*DIRS[d]))
            def _():
                kinds[name](d).wait_send()

    for load in loads:
        load.wait()
    pl.semaphore_wait(barrier, near_x * near_y - 1)
    send("k")
    send("p")
    send("s")

    def clear(ref, *index):
        view = ref.at[index]
        view[...] = jnp.zeros(view.shape, f32)

    for ref, halo, wide, corner in ((ke, khalo, 3, 2), (pe, phalo, 3, 2), (se, shalo, 2, 1)):
        for at in (slice(0, 3 - corner), slice(19 + corner, 22)):
            clear(halo, slice(0, 2), at)
        if wide < 3:
            clear(ref, slice(0, 1))
            clear(ref, slice(21, 22))
    for dx, dy in DIRS:
        @pl.when(jnp.logical_not(exists(-dx, -dy)))
        def _():
            for ref, halo, wide, corner in (
                (ke, khalo, 3, 2), (pe, phalo, 3, 2), (se, shalo, 2, 1), (rr, None, 1, 0),
            ):
                if dy == 0:
                    at = slice(3 - wide, 3) if dx > 0 else slice(19, 19 + wide)
                    clear(ref, at, slice(0, 16))
                else:
                    lo, hi = {0: (3, 19), 1: (3 - corner, 3), -1: (19, 19 + corner)}[dx]
                    if halo is not None:
                        clear(halo, FROM[dy] - 1, slice(lo, hi))
                    elif dx == 0:
                        clear(rhalo, FROM[dy] - 1)
            part = {0: cm, 1: cl, -1: cr}[dx]
            clear(part, FROM[dy])

    low_half = lax.broadcasted_iota(jnp.int32, (8, 256), 0) < 4
    y_at = lax.broadcasted_iota(jnp.int32, (24, 256), 0)
    z_at = lax.broadcasted_iota(jnp.int32, (24, 256), 1)
    y_rel = jnp.where(y_at < 20, y_at, y_at - 24)
    y_glob = y_rel + row * width
    ends_yz = (
        (y_glob == 0).astype(f32) + (y_glob == rows * width - 1).astype(f32)
        + (z_at == 0).astype(f32) + (z_at == 255).astype(f32)
    )
    odd_y = (y_at & 1) == 1
    odd_z = (z_at & 1) == 1

    def loop(lo, hi, step, unroll=4):
        def run(i, carry):
            step(i)
            return carry
        lax.fori_loop(lo, hi, run, 0, unroll=unroll)

    def set_rim(body, halo, lo, hi):
        def step(i):
            body[i, 16:24] = jnp.where(low_half, halo[1, i], halo[0, i])
        loop(lo, hi, step)

    def next_y(v):
        return pltpu.roll(v, 23, 0)

    def prev_y(v):
        return pltpu.roll(v, 1, 0)

    def next_z(v):
        return pltpu.roll(v, 255, 1)

    def prev_z(v):
        return pltpu.roll(v, 1, 1)

    def face(a, b):
        total = a + b
        return 2.0 * a * b / jnp.where(total > 0, total, 1.0)

    ids = [agg[slab * width + x] for x in range(width)]
    slots = [i - ids[0] for i in ids]
    live = slots[15]
    col = lax.broadcasted_iota(jnp.int32, (1, 256), 1)
    slot_col = jnp.zeros((1, 256), jnp.int32)
    for x in range(width):
        inside = (col >> 4) == x
        slot_col = jnp.where(inside, slots[x], slot_col)
    r168 = lax.broadcasted_iota(jnp.int32, (168, 256), 0)
    c168 = lax.broadcasted_iota(jnp.int32, (168, 256), 1)
    want = jnp.where(r168 < 128, r168 >> 3, (r168 >> 3) - 20 + live)
    gather = ((want == slot_col) & ((r168 & 7) == ((c168 & 15) >> 1))).astype(f32)
    gather = jnp.concatenate([gather, gather], axis=1).astype(jnp.bfloat16)
    zr = lax.broadcasted_iota(jnp.int32, (512, 128), 0)
    zc = lax.broadcasted_iota(jnp.int32, (512, 128), 1)
    pair_z = (((zr & 255) >> 1) == zc).astype(f32).astype(jnp.bfloat16)

    def coarsen(q0, q1):
        count = q1 - q0
        flat = fields[q0:q1].reshape(count * 256, 256)
        pairs = dot(jnp.concatenate(halves(flat), axis=1), pair_z)
        pairs = jnp.concatenate([pairs[256 * q:256 * (q + 1)] for q in range(count)], axis=1)
        sums = dot(gather, jnp.concatenate(halves(pairs), axis=0))
        for q in range(count):
            part = sums[:, 128 * q:128 * (q + 1)]
            cm[0, q0 + q] = part[0:128]
            cs[q0 + q] = part[128:168]

    receive("k")
    set_rim(ke, khalo, 0, 22)

    def x_faces(i):
        fx[i] = face(ke[i], ke[i + 1])
    loop(0, 21, x_faces)

    def other_faces(i):
        k = ke[i]
        north = face(k, next_y(k))
        above = jnp.where(z_at == 255, 0.0, face(k, next_z(k)))
        south, below = prev_y(north), prev_z(above)
        x_glob = slab * width + i - 3
        ends_x = (x_glob == 0).astype(f32) + (x_glob == slabs * width - 1).astype(f32)
        bound = 2.0 * k * (ends_yz + ends_x)
        fy[i] = north
        fz[i] = above
        diag = fx[i - 1] + fx[i] + north + south + above + below + bound
        dg[i] = diag
        wt[i] = OMEGA / jnp.where(diag > 0, diag, 1.0)
        return north, above, south, below, bound

    def plain_faces(i):
        other_faces(i)

    def own_faces(i):
        north, above, south, below, bound = other_faces(i)
        x = slab * width + i - 3
        crossing = agg[x] != agg[jnp.minimum(x + 1, slabs * width - 1)]
        fields[1, i - 3] = fx[i, 0:16] * crossing.astype(f32)
        fields[2, i - 3] = jnp.where(odd_y, north, 0.0)[0:16]
        fields[3, i - 3] = jnp.where(odd_z, above, 0.0)[0:16]
        whole = bound + jnp.where(odd_y, north, south) + jnp.where(odd_z, above, below)
        fields[4, i - 3] = whole[0:16]

    loop(3, 19, own_faces)
    coarsen(1, 5)
    send("coef")
    loop(1, 3, plain_faces)
    loop(19, 21, plain_faces)

    def beside(src, i):
        v = src[i]
        north, above = fy[i], fz[i]
        around = fx[i - 1] * src[i - 1] + fx[i] * src[i + 1]
        around = around + (north * next_y(v) + prev_y(north * v))
        return v, around + (above * next_z(v) + prev_z(above * v))

    def sweep(src, dst, lo, hi):
        def step(i):
            v, around = beside(src, i)
            dst[i] = (1.0 - OMEGA) * v + wt[i] * (se[i] + around)
        loop(lo, hi, step)

    receive("p")
    set_rim(pe, phalo, 0, 22)
    receive("s")
    set_rim(se, shalo, 1, 21)
    sweep(pe, p1, 1, 21)
    sweep(p1, p2, 2, 20)

    def residual(i):
        v, around = beside(p2, i)
        fields[0, i - 3] = (se[i] - dg[i] * v + around)[0:16]
    loop(3, 19, residual)
    coarsen(0, 1)
    send("rhs")

    rp = lax.broadcasted_iota(jnp.int32, (384, 64), 0)
    cp = lax.broadcasted_iota(jnp.int32, (384, 64), 1)
    place = (((rp >> 4) - (cp >> 4) == 4 + live) & ((rp & 15) == (cp & 15))).astype(f32)
    place = jnp.concatenate([place, place], axis=1).astype(jnp.bfloat16)
    low_coarse = lax.broadcasted_iota(jnp.int32, (1, 8, 128), 1) < 4

    def joined(part, q, count):
        own = part[0, q].reshape(count, 8, 128)
        below = part[1, q].reshape(count, 8, 128)
        above = part[2, q].reshape(count, 8, 128)
        return jnp.concatenate([own, jnp.where(low_coarse, above, below)], axis=1)

    def extend(q0, q1):
        count = q1 - q0
        ahead = [joined(cr, q, 4).reshape(64, 128) for q in range(q0, q1)]
        after = dot(place, jnp.concatenate(halves(jnp.concatenate(ahead, axis=1)), axis=0))
        for q in range(q0, q1):
            at = 128 * (q - q0)
            ext[q] = after[:, at:at + 128].reshape(24, 16, 128)
            ext[q, 0:5] += joined(cl, q, 5)
            ext[q, 4:20] += joined(cm, q, 16)

    receive("coef")
    extend(1, 5)
    zl = lax.broadcasted_iota(jnp.int32, (16, 128), 1)
    def diagonal(t):
        diag = ext[4, t] + ext[1, t] + ext[1, t - 1]
        corr[2, t] = OMEGA / jnp.where(diag > 0, diag, 1.0)
    loop(1, 23, diagonal)
    receive("rhs")
    extend(0, 1)

    def first(t):
        corr[0, t] = corr[2, t] * ext[0, t]
    loop(1, 23, first)
    for number, (lo, hi) in enumerate(((2, 22), (3, 21), (4, 20))):
        src, dst = number % 2, (number + 1) % 2
        def coarse_sweep(t):
            v = corr[src, t]
            north, above = ext[2, t], ext[3, t]
            around = ext[1, t] * corr[src, t + 1] + ext[1, t - 1] * corr[src, t - 1]
            around = around + (north * pltpu.roll(v, 15, 0) + pltpu.roll(north * v, 1, 0))
            around = around + (above * pltpu.roll(v, 127, 1) + pltpu.roll(above * v, 1, 1))
            corr[dst, t] = (1.0 - OMEGA) * v + corr[2, t] * (ext[0, t] + around)
        loop(lo, hi, coarse_sweep)

    ru = lax.broadcasted_iota(jnp.int32, (24, 256), 0)
    cu = lax.broadcasted_iota(jnp.int32, (24, 256), 1)
    same_y = (cu & 15) == jnp.where(ru < 20, ru >> 1, (ru >> 1) + 4)
    spread = jnp.concatenate(
        [(same_y & ((cu >> 4) == slots[x])).astype(f32) for x in range(width)], axis=0
    )
    er = lax.broadcasted_iota(jnp.int32, (256, 256), 0)
    ec = lax.broadcasted_iota(jnp.int32, (256, 256), 1)
    twice_z = ((ec >> 1) == (er & 127)).astype(f32).astype(jnp.bfloat16)
    coarse = jnp.concatenate(halves(corr[1, 4:20].reshape(256, 128)), axis=1)
    fine = dot(dot(spread.astype(jnp.bfloat16), coarse).astype(jnp.bfloat16), twice_z)
    fine = fine.reshape(16, 24, 256)
    p1[3:19] = p2[3:19] + fine
    p1[2] = p2[2] + fine[0]
    p1[19] = p2[19] + fine[15]
    sweep(p1, rr, 3, 19)
    edge[0] = rr[3:19, 15, :]
    edge[1] = rr[3:19, 0, :]
    send("post")
    receive("post")
    for i in range(16):
        rr[i + 3, 23:24] = rhalo[0, i:i + 1]
        rr[i + 3, 16:17] = rhalo[1, i:i + 1]

    def last(i):
        v, around = beside(rr, i)
        result[i - 3] = ((1.0 - OMEGA) * v + wt[i] * (se[i] + around))[0:16]
    loop(3, 19, last)
    store = pltpu.make_async_copy(result, out, local_sem.at[0])
    store.start()
    for name in kinds:
        sent(name)
    store.wait()


def body(permeability, source, pressure, aggregate):
    f32 = jnp.float32
    shape = permeability.shape
    block = pltpu.VMEM((22, 24, 256), f32)
    halo = pltpu.VMEM((2, 22, 8, 256), f32)
    hbm = pl.BlockSpec(memory_space=pl.ANY)
    return pl.pallas_call(
        kernel,
        out_shape=jax.ShapeDtypeStruct(shape, f32),
        in_specs=[pl.BlockSpec(memory_space=pltpu.SMEM), hbm, hbm, hbm],
        out_specs=hbm,
        scratch_shapes=[block, block, block, halo, halo, halo]
        + [block] * 8
        + [
            pltpu.VMEM((2, 16, 256), f32),
            pltpu.VMEM((2, 16, 256), f32),
            pltpu.VMEM((16, 16, 256), f32),
            pltpu.VMEM((5, 16, 16, 256), f32),
            pltpu.VMEM((3, 5, 128, 128), f32),
            pltpu.VMEM((3, 5, 40, 128), f32),
            pltpu.VMEM((3, 5, 32, 128), f32),
            pltpu.VMEM((5, 40, 128), f32),
            pltpu.VMEM((5, 24, 16, 128), f32),
            pltpu.VMEM((3, 24, 16, 128), f32),
            pltpu.SemaphoreType.DMA((3,)),
            pltpu.SemaphoreType.DMA((48,)),
            pltpu.SemaphoreType.DMA((48,)),
        ],
        compiler_params=pltpu.CompilerParams(
            collective_id=0, has_side_effects=True, vmem_limit_bytes=62 * 2**20
        ),
    )(aggregate, permeability, source, pressure)


def solution(mesh):
    spec = P(("real", "slab"), ("pencil", "sub"), None)
    return jax.shard_map(
        body, mesh=mesh, in_specs=(spec, spec, spec, P("real")), out_specs=spec, check_vma=False
    )
```

```python
import functools
import jax
import jax.numpy as jnp
from jax import lax
from jax.experimental import pallas as pl
from jax.experimental.pallas import tpu as pltpu
from jax.sharding import PartitionSpec as P

OMEGA = 0.8
GRANT = 62 * 2**20
MESH = pl.DeviceIdType.MESH

DIRS = [(dx, dy) for dx in (1, 0, -1) for dy in (1, 0, -1) if (dx, dy) != (0, 0)]
FROM = {0: 0, 1: 1, -1: 2}


def dot(a, b):
    return jnp.dot(a, b, preferred_element_type=jnp.float32)


def halves(v):
    upper = v.astype(jnp.bfloat16)
    return upper, (v - upper.astype(jnp.float32)).astype(jnp.bfloat16)


def kernel(
    agg, k_in, s_in, p_in, out,
    ke, se, pe, khalo, shalo, phalo, fx, fy, fz, dg, wt, p1, p2, rr, rhalo,
    kpack, ppack, spack, edge, result, fields, cm, cl, cr, cs, cmp, csp, hm, hl, hr, ext, corr, local_sem, send_sem, recv_sem,
):
    f32 = jnp.float32
    width = 16
    slab, slabs = lax.axis_index("slab"), lax.axis_size("slab")
    subs = lax.axis_size("sub")
    rows = lax.axis_size("pencil") * subs
    row = lax.axis_index("pencil") * subs + lax.axis_index("sub")

    loads = [
        pltpu.make_async_copy(src, dst.at[3:19, 0:16], local_sem.at[i])
        for i, (src, dst) in enumerate(((k_in, ke), (p_in, pe), (s_in, se)))
    ]
    for load in loads:
        load.start()

    def exists(dx, dy):
        ok = None
        for pos, step, count in ((slab, dx, slabs), (row, dy, rows)):
            if step:
                here = (pos + step < count) if step > 0 else (pos > 0)
                ok = here if ok is None else jnp.logical_and(ok, here)
        return ok

    def device(dx, dy):
        r = row + dy
        return {"slab": slab + dx, "pencil": r // subs, "sub": r % subs}

    barrier = pltpu.get_barrier_semaphore()
    for dx, dy in DIRS:
        @pl.when(exists(dx, dy))
        def _():
            pl.semaphore_signal(barrier, inc=1, device_id=device(dx, dy), device_id_type=MESH)
    near_x = 1 + (slab > 0).astype(jnp.int32) + (slab < slabs - 1).astype(jnp.int32)
    near_y = 1 + (row > 0).astype(jnp.int32) + (row < rows - 1).astype(jnp.int32)

    def message(kind, d, src, dst):
        return pltpu.make_async_remote_copy(
            src_ref=src, dst_ref=dst,
            send_sem=send_sem.at[kind * 8 + d], recv_sem=recv_sem.at[kind * 8 + d],
            device_id=device(*DIRS[d]), device_id_type=MESH,
        )

    def fine_message(kind, d, body, packed, halo, wide):
        dx, dy = DIRS[d]
        if dy == 0:
            src0 = 19 - wide if dx > 0 else 3
            dst0 = 3 - wide if dx > 0 else 19
            return message(kind, d, body.at[src0:src0 + wide, 0:16], body.at[dst0:dst0 + wide, 0:16])
        src0, dst0, length = {0: (1, 1, 8), 1: (9, 0, 1), -1: (0, 9, 1)}[dx]
        return message(
            kind, d, packed.at[FROM[dy] - 1, src0:src0 + length],
            halo.at[FROM[dy] - 1, dst0:dst0 + length],
        )

    def coarse_message(kind, d, q0, q1):
        dx, dy = DIRS[d]
        if dy == 0:
            qs = pl.ds(q0, q1 - q0)
            if dx > 0:
                return message(kind, d, cs.at[qs], cl.at[qs])
            return message(kind, d, cm.at[qs, 0:32], cr.at[qs])
        here = FROM[dy] - 1
        if q0 == 0:
            if dx > 0:
                return message(kind, d, cs.at[0], hl.at[here, 2])
            if dx < 0:
                return message(kind, d, cm.at[0, 0:32], hr.at[here, 2])
            return message(kind, d, cmp.at[here, 2, 0:64], hm.at[here, 2, 0:64])
        if dx > 0:
            return message(kind, d, csp.at[here], hl.at[here, 0:2])
        if dx < 0:
            return message(kind, d, cmp.at[here, 0:2, 0:32], hr.at[here, 0:2])
        return message(kind, d, cmp.at[here, 0:2], hm.at[here, 0:2])

    def post_message(d):
        dx, dy = DIRS[d]
        if dy == 0:
            return fine_message(5, d, rr, None, None, 1)
        return message(5, d, edge.at[FROM[dy] - 1], rhalo.at[FROM[dy] - 1])

    kinds = {
        "k": lambda d: fine_message(0, d, ke, kpack, khalo, 3),
        "p": lambda d: fine_message(1, d, pe, ppack, phalo, 3),
        "s": lambda d: fine_message(2, d, se, spack, shalo, 2),
        "coef": lambda d: coarse_message(3, d, 1, 5),
        "rhs": lambda d: coarse_message(4, d, 0, 1),
        "post": post_message,
    }

    def each(name):
        return [d for d in range(8) if name != "post" or 0 in DIRS[d]]

    def send(name):
        for d in each(name):
            @pl.when(exists(*DIRS[d]))
            def _():
                kinds[name](d).start()

    def receive(name):
        for d in each(name):
            dx, dy = DIRS[d]
            @pl.when(exists(-dx, -dy))
            def _():
                kinds[name](d).wait_recv()

    def sent(name):
        for d in each(name):
            @pl.when(exists(*DIRS[d]))
            def _():
                kinds[name](d).wait_send()

    low_half = lax.broadcasted_iota(jnp.int32, (1, 8, 256), 1) < 4
    low_coarse = lax.broadcasted_iota(jnp.int32, (1, 8, 128), 1) < 4

    def turned(v):
        return pltpu.roll(v, 4, 1)

    def pair_up(a, b, low):
        return jnp.where(low, turned(b), a), jnp.where(low, a, turned(b))

    def pair_off(up, down, low):
        return jnp.where(low, down, up), turned(jnp.where(low, up, down))

    def pack(body, packed):
        for at, a, b, count in ((1, 3, 11, 8), (0, 3, 4, 1), (9, 17, 18, 1)):
            for way, lo in ((0, 8), (1, 0)):
                tiles = pair_up(body[a:a + count, lo:lo + 8], body[b:b + count, lo:lo + 8], low_half)
                packed[way, at:at + count] = tiles[way]

    for load, parts in zip(loads, ((ke, kpack), (pe, ppack), (se, spack))):
        load.wait()
        pack(*parts)
    pl.semaphore_wait(barrier, near_x * near_y - 1)
    send("k")
    send("p")
    send("s")

    def clear(ref, *index):
        view = ref.at[index]
        view[...] = jnp.zeros(view.shape, f32)

    for ref in (ke, pe):
        clear(ref, 0, slice(16, 24))
        clear(ref, 21, slice(16, 24))
    for dx, dy in DIRS:
        @pl.when(jnp.logical_not(exists(-dx, -dy)))
        def _():
            for ref, halo, wide in (
                (ke, khalo, 3), (pe, phalo, 3), (se, shalo, 2), (rr, None, 1),
            ):
                if dy == 0:
                    at = slice(3 - wide, 3) if dx > 0 else slice(19, 19 + wide)
                    clear(ref, at, slice(0, 16))
                else:
                    lo, hi = {0: (1, 9), 1: (0, 1), -1: (9, 10)}[dx]
                    if halo is not None:
                        clear(halo, FROM[dy] - 1, slice(lo, hi))
                    elif dx == 0:
                        clear(rhalo, FROM[dy] - 1)
            if dy == 0:
                clear({1: cl, -1: cr}[dx])
            else:
                clear({0: hm, 1: hl, -1: hr}[dx], FROM[dy] - 1)

    y_at = lax.broadcasted_iota(jnp.int32, (24, 256), 0)
    z_at = lax.broadcasted_iota(jnp.int32, (24, 256), 1)
    y_rel = jnp.where(y_at < 20, y_at, y_at - 24)
    y_glob = y_rel + row * width
    ends_yz = (
        (y_glob == 0).astype(f32) + (y_glob == rows * width - 1).astype(f32)
        + (z_at == 0).astype(f32) + (z_at == 255).astype(f32)
    )
    odd_y = (y_at & 1) == 1
    odd_z = (z_at & 1) == 1

    def loop(lo, hi, step, unroll=4):
        def run(i, carry):
            step(i)
            return carry
        lax.fori_loop(lo, hi, run, 0, unroll=unroll)

    def set_rim(body, halo):
        for at, a, b, count in ((1, 3, 11, 8), (0, 1, 2, 1), (9, 19, 20, 1)):
            here = slice(at, at + count)
            first, second = pair_off(halo[0, here], halo[1, here], low_half)
            body[a:a + count, 16:24] = first
            body[b:b + count, 16:24] = second

    def next_y(v):
        return pltpu.roll(v, 23, 0)

    def prev_y(v):
        return pltpu.roll(v, 1, 0)

    def next_z(v):
        return pltpu.roll(v, 255, 1)

    def prev_z(v):
        return pltpu.roll(v, 1, 1)

    def face(a, b):
        total = a + b
        return 2.0 * a * b / jnp.where(total > 0, total, 1.0)

    ids = [agg[slab * width + x] for x in range(width)]
    slots = [i - ids[0] for i in ids]
    live = slots[15]
    col = lax.broadcasted_iota(jnp.int32, (1, 256), 1)
    slot_col = jnp.zeros((1, 256), jnp.int32)
    for x in range(width):
        inside = (col >> 4) == x
        slot_col = jnp.where(inside, slots[x], slot_col)
    r168 = lax.broadcasted_iota(jnp.int32, (168, 256), 0)
    c168 = lax.broadcasted_iota(jnp.int32, (168, 256), 1)
    want = jnp.where(r168 < 128, r168 >> 3, (r168 >> 3) - 20 + live)
    gather = ((want == slot_col) & ((r168 & 7) == ((c168 & 15) >> 1))).astype(f32)
    gather = jnp.concatenate([gather, gather], axis=1).astype(jnp.bfloat16)
    zr = lax.broadcasted_iota(jnp.int32, (512, 128), 0)
    zc = lax.broadcasted_iota(jnp.int32, (512, 128), 1)
    pair_z = (((zr & 255) >> 1) == zc).astype(f32).astype(jnp.bfloat16)

    def coarsen(q0, q1):
        count = q1 - q0
        flat = fields[q0:q1].reshape(count * 256, 256)
        pairs = dot(jnp.concatenate(halves(flat), axis=1), pair_z)
        pairs = jnp.concatenate([pairs[256 * q:256 * (q + 1)] for q in range(count)], axis=1)
        sums = dot(gather, jnp.concatenate(halves(pairs), axis=0))
        for q in range(count):
            part = sums[:, 128 * q:128 * (q + 1)]
            cm[q0 + q] = part[0:128]
            cs[q0 + q] = part[128:168]

    def pack_coarse(packed, pair, a, b):
        tiles = pair_up(a.reshape(-1, 8, 128), b.reshape(-1, 8, 128), low_coarse)
        for way in range(2):
            packed[way, pair, 0:a.shape[0]] = tiles[way].reshape(a.shape)

    receive("k")
    set_rim(ke, khalo)

    def x_faces(i):
        fx[i] = face(ke[i], ke[i + 1])
    loop(0, 21, x_faces)

    def other_faces(i):
        k = ke[i]
        north = face(k, next_y(k))
        above = jnp.where(z_at == 255, 0.0, face(k, next_z(k)))
        south, below = prev_y(north), prev_z(above)
        x_glob = slab * width + i - 3
        ends_x = (x_glob == 0).astype(f32) + (x_glob == slabs * width - 1).astype(f32)
        bound = 2.0 * k * (ends_yz + ends_x)
        fy[i] = north
        fz[i] = above
        diag = fx[i - 1] + fx[i] + north + south + above + below + bound
        dg[i] = diag
        wt[i] = OMEGA / jnp.where(diag > 0, diag, 1.0)
        return north, above, south, below, bound

    def plain_faces(i):
        other_faces(i)

    def own_faces(i):
        north, above, south, below, bound = other_faces(i)
        x = slab * width + i - 3
        crossing = agg[x] != agg[jnp.minimum(x + 1, slabs * width - 1)]
        fields[1, i - 3] = fx[i, 0:16] * crossing.astype(f32)
        fields[2, i - 3] = jnp.where(odd_y, north, 0.0)[0:16]
        fields[3, i - 3] = jnp.where(odd_z, above, 0.0)[0:16]
        whole = bound + jnp.where(odd_y, north, south) + jnp.where(odd_z, above, below)
        fields[4, i - 3] = whole[0:16]

    loop(3, 19, own_faces)
    coarsen(1, 5)
    for pair, q in ((0, 1), (1, 3)):
        pack_coarse(cmp, pair, cm[q], cm[q + 1])
        pack_coarse(csp, pair, cs[q], cs[q + 1])
    send("coef")
    loop(1, 3, plain_faces)
    loop(19, 21, plain_faces)

    def beside(src, i):
        v = src[i]
        north, above = fy[i], fz[i]
        around = fx[i - 1] * src[i - 1] + fx[i] * src[i + 1]
        around = around + (north * next_y(v) + prev_y(north * v))
        return v, around + (above * next_z(v) + prev_z(above * v))

    def sweep(src, dst, lo, hi):
        def step(i):
            v, around = beside(src, i)
            dst[i] = (1.0 - OMEGA) * v + wt[i] * (se[i] + around)
        loop(lo, hi, step)

    receive("p")
    set_rim(pe, phalo)
    receive("s")
    set_rim(se, shalo)
    sweep(pe, p1, 1, 21)
    sweep(p1, p2, 2, 20)

    def residual(i):
        v, around = beside(p2, i)
        fields[0, i - 3] = (se[i] - dg[i] * v + around)[0:16]
    loop(3, 19, residual)
    coarsen(0, 1)
    pack_coarse(cmp, 2, cm[0, 0:64], cm[0, 64:128])
    send("rhs")

    rp = lax.broadcasted_iota(jnp.int32, (384, 64), 0)
    cp = lax.broadcasted_iota(jnp.int32, (384, 64), 1)
    place = (((rp >> 4) - (cp >> 4) == 4 + live) & ((rp & 15) == (cp & 15))).astype(f32)
    place = jnp.concatenate([place, place], axis=1).astype(jnp.bfloat16)

    def joined(part, halo, q, count):
        own = part[q].reshape(count, 8, 128)
        if q > 0:
            pair = (q - 1) // 2
            tiles = [halo[way, pair].reshape(count, 8, 128) for way in range(2)]
            rim = pair_off(*tiles, low_coarse)[(q - 1) % 2]
        elif count == 16:
            tiles = [halo[way, 2, 0:64].reshape(8, 8, 128) for way in range(2)]
            rim = jnp.concatenate(pair_off(*tiles, low_coarse), axis=0)
        else:
            tiles = [halo[way, 2].reshape(count, 8, 128) for way in range(2)]
            rim = pair_off(*tiles, low_coarse)[0]
        return jnp.concatenate([own, rim], axis=1)

    def extend(q0, q1):
        count = q1 - q0
        ahead = [joined(cr, hr, q, 4).reshape(64, 128) for q in range(q0, q1)]
        after = dot(place, jnp.concatenate(halves(jnp.concatenate(ahead, axis=1)), axis=0))
        for q in range(q0, q1):
            at = 128 * (q - q0)
            ext[q] = after[:, at:at + 128].reshape(24, 16, 128)
            ext[q, 0:5] += joined(cl, hl, q, 5)
            ext[q, 4:20] += joined(cm, hm, q, 16)

    receive("coef")
    extend(1, 5)
    zl = lax.broadcasted_iota(jnp.int32, (16, 128), 1)
    def diagonal(t):
        diag = ext[4, t] + ext[1, t] + ext[1, t - 1]
        corr[2, t] = OMEGA / jnp.where(diag > 0, diag, 1.0)
    loop(1, 23, diagonal)
    receive("rhs")
    extend(0, 1)

    def first(t):
        corr[0, t] = corr[2, t] * ext[0, t]
    loop(1, 23, first)
    for number, (lo, hi) in enumerate(((2, 22), (3, 21), (4, 20))):
        src, dst = number % 2, (number + 1) % 2
        def coarse_sweep(t):
            v = corr[src, t]
            north, above = ext[2, t], ext[3, t]
            around = ext[1, t] * corr[src, t + 1] + ext[1, t - 1] * corr[src, t - 1]
            around = around + (north * pltpu.roll(v, 15, 0) + pltpu.roll(north * v, 1, 0))
            around = around + (above * pltpu.roll(v, 127, 1) + pltpu.roll(above * v, 1, 1))
            corr[dst, t] = (1.0 - OMEGA) * v + corr[2, t] * (ext[0, t] + around)
        loop(lo, hi, coarse_sweep)

    ru = lax.broadcasted_iota(jnp.int32, (24, 256), 0)
    cu = lax.broadcasted_iota(jnp.int32, (24, 256), 1)
    same_y = (cu & 15) == jnp.where(ru < 20, ru >> 1, (ru >> 1) + 4)
    spread = jnp.concatenate(
        [(same_y & ((cu >> 4) == slots[x])).astype(f32) for x in range(width)], axis=0
    )
    er = lax.broadcasted_iota(jnp.int32, (256, 256), 0)
    ec = lax.broadcasted_iota(jnp.int32, (256, 256), 1)
    twice_z = ((ec >> 1) == (er & 127)).astype(f32).astype(jnp.bfloat16)
    coarse = jnp.concatenate(halves(corr[1, 4:20].reshape(256, 128)), axis=1)
    fine = dot(dot(spread.astype(jnp.bfloat16), coarse).astype(jnp.bfloat16), twice_z)
    fine = fine.reshape(16, 24, 256)
    p1[3:19] = p2[3:19] + fine
    p1[2] = p2[2] + fine[0]
    p1[19] = p2[19] + fine[15]
    sweep(p1, rr, 3, 19)
    edge[0] = rr[3:19, 15, :]
    edge[1] = rr[3:19, 0, :]
    send("post")
    receive("post")
    for i in range(16):
        rr[i + 3, 23:24] = rhalo[0, i:i + 1]
        rr[i + 3, 16:17] = rhalo[1, i:i + 1]

    def last(i):
        v, around = beside(rr, i)
        result[i - 3] = ((1.0 - OMEGA) * v + wt[i] * (se[i] + around))[0:16]
    loop(3, 19, last)
    store = pltpu.make_async_copy(result, out, local_sem.at[0])
    store.start()
    for name in kinds:
        sent(name)
    store.wait()


def store_kernel(field, out, sem):
    step = field.shape[0] // 8
    stores = [
        pltpu.make_async_copy(field.at[at:at + step], out.at[at:at + step], sem.at[at // step])
        for at in range(0, field.shape[0], step)
    ]
    for store in stores:
        store.start()
    for store in stores:
        store.wait()


def body(permeability, source, pressure, aggregate):
    f32 = jnp.float32
    shape = permeability.shape
    block = pltpu.VMEM((22, 24, 256), f32)
    halo = pltpu.VMEM((2, 10, 8, 256), f32)
    hbm = pl.BlockSpec(memory_space=pltpu.HBM)
    result = pl.pallas_call(
        kernel,
        out_shape=jax.ShapeDtypeStruct(shape, f32),
        in_specs=[pl.BlockSpec(memory_space=pltpu.SMEM), hbm, hbm, hbm],
        out_specs=hbm,
        scratch_shapes=[block, block, block, halo, halo, halo]
        + [block] * 8
        + [
            pltpu.VMEM((2, 16, 256), f32),
            halo,
            halo,
            halo,
            pltpu.VMEM((2, 16, 256), f32),
            pltpu.VMEM((16, 16, 256), f32),
            pltpu.VMEM((5, 16, 16, 256), f32),
            pltpu.VMEM((5, 128, 128), f32),
            pltpu.VMEM((5, 40, 128), f32),
            pltpu.VMEM((5, 32, 128), f32),
            pltpu.VMEM((5, 40, 128), f32),
            pltpu.VMEM((2, 3, 128, 128), f32),
            pltpu.VMEM((2, 2, 40, 128), f32),
            pltpu.VMEM((2, 3, 128, 128), f32),
            pltpu.VMEM((2, 3, 40, 128), f32),
            pltpu.VMEM((2, 3, 32, 128), f32),
            pltpu.VMEM((5, 24, 16, 128), f32),
            pltpu.VMEM((3, 24, 16, 128), f32),
            pltpu.SemaphoreType.DMA((3,)),
            pltpu.SemaphoreType.DMA((48,)),
            pltpu.SemaphoreType.DMA((48,)),
        ],
        compiler_params=pltpu.CompilerParams(
            collective_id=0, has_side_effects=True, vmem_limit_bytes=GRANT
        ),
    )(aggregate, permeability, source, pressure)
    return pl.pallas_call(
        store_kernel,
        out_shape=jax.ShapeDtypeStruct(shape, f32),
        in_specs=[hbm],
        out_specs=hbm,
        scratch_shapes=[pltpu.SemaphoreType.DMA((8,))],
        compiler_params=pltpu.CompilerParams(vmem_limit_bytes=GRANT),
    )(result)


def solution(mesh):
    spec = P(("real", "slab"), ("pencil", "sub"), None)
    return jax.shard_map(
        body, mesh=mesh, in_specs=(spec, spec, spec, P("real")), out_specs=spec, check_vma=False
    )
```

```python
import functools
import jax
import jax.numpy as jnp
from jax import lax
from jax.experimental import pallas as pl
from jax.experimental.pallas import tpu as pltpu
from jax.sharding import PartitionSpec as P

OMEGA = 0.8
GRANT = 50 * 2**20
MESH = pl.DeviceIdType.MESH

DIRS = [(dx, dy) for dx in (1, 0, -1) for dy in (1, 0, -1) if (dx, dy) != (0, 0)]
FROM = {0: 0, 1: 1, -1: 2}


def dot(a, b):
    return jnp.dot(a, b, preferred_element_type=jnp.float32)


def halves(v):
    upper = v.astype(jnp.bfloat16)
    return upper, (v - upper.astype(jnp.float32)).astype(jnp.bfloat16)


def kernel(
    agg, k_in, s_in, p_in, out,
    ke, se, pe, khalo, shalo, phalo, fx, fy, fz, dg, wt, p1, p2, rr, rhalo,
    kpack, ppack, spack, edge, fields, cm, cl, cr, cs, cmp, csp, hm, hl, hr, ext, corr, local_sem, send_sem, recv_sem,
):
    f32 = jnp.float32
    width = 16
    slab, slabs = lax.axis_index("slab"), lax.axis_size("slab")
    subs = lax.axis_size("sub")
    rows = lax.axis_size("pencil") * subs
    row = lax.axis_index("pencil") * subs + lax.axis_index("sub")

    loads = [
        pltpu.make_async_copy(src, dst.at[3:19, 0:16], local_sem.at[i])
        for i, (src, dst) in enumerate(((k_in, ke), (p_in, pe), (s_in, se)))
    ]
    for load in loads:
        load.start()

    def exists(dx, dy):
        ok = None
        for pos, step, count in ((slab, dx, slabs), (row, dy, rows)):
            if step:
                here = (pos + step < count) if step > 0 else (pos > 0)
                ok = here if ok is None else jnp.logical_and(ok, here)
        return ok

    def device(dx, dy):
        r = row + dy
        return {"slab": slab + dx, "pencil": r // subs, "sub": r % subs}

    barrier = pltpu.get_barrier_semaphore()
    for dx, dy in DIRS:
        @pl.when(exists(dx, dy))
        def _():
            pl.semaphore_signal(barrier, inc=1, device_id=device(dx, dy), device_id_type=MESH)
    near_x = 1 + (slab > 0).astype(jnp.int32) + (slab < slabs - 1).astype(jnp.int32)
    near_y = 1 + (row > 0).astype(jnp.int32) + (row < rows - 1).astype(jnp.int32)

    def message(kind, d, src, dst):
        return pltpu.make_async_remote_copy(
            src_ref=src, dst_ref=dst,
            send_sem=send_sem.at[kind * 8 + d], recv_sem=recv_sem.at[kind * 8 + d],
            device_id=device(*DIRS[d]), device_id_type=MESH,
        )

    def fine_message(kind, d, body, packed, halo, wide):
        dx, dy = DIRS[d]
        if dy == 0:
            src0 = 19 - wide if dx > 0 else 3
            dst0 = 3 - wide if dx > 0 else 19
            return message(kind, d, body.at[src0:src0 + wide, 0:16], body.at[dst0:dst0 + wide, 0:16])
        src0, dst0, length = {0: (1, 1, 8), 1: (9, 0, 1), -1: (0, 9, 1)}[dx]
        return message(
            kind, d, packed.at[FROM[dy] - 1, src0:src0 + length],
            halo.at[FROM[dy] - 1, dst0:dst0 + length],
        )

    def coarse_message(kind, d, q0, q1):
        dx, dy = DIRS[d]
        if dy == 0:
            qs = pl.ds(q0, q1 - q0)
            if dx > 0:
                return message(kind, d, cs.at[qs], cl.at[qs])
            return message(kind, d, cm.at[qs, 0:32], cr.at[qs])
        here = FROM[dy] - 1
        if q0 == 0:
            if dx > 0:
                return message(kind, d, cs.at[0], hl.at[here, 2])
            if dx < 0:
                return message(kind, d, cm.at[0, 0:32], hr.at[here, 2])
            return message(kind, d, cmp.at[here, 2, 0:64], hm.at[here, 2, 0:64])
        if dx > 0:
            return message(kind, d, csp.at[here], hl.at[here, 0:2])
        if dx < 0:
            return message(kind, d, cmp.at[here, 0:2, 0:32], hr.at[here, 0:2])
        return message(kind, d, cmp.at[here, 0:2], hm.at[here, 0:2])

    def post_message(d):
        dx, dy = DIRS[d]
        if dy == 0:
            return fine_message(5, d, rr, None, None, 1)
        return message(5, d, edge.at[FROM[dy] - 1], rhalo.at[FROM[dy] - 1])

    kinds = {
        "k": lambda d: fine_message(0, d, ke, kpack, khalo, 3),
        "p": lambda d: fine_message(1, d, pe, ppack, phalo, 3),
        "s": lambda d: fine_message(2, d, se, spack, shalo, 2),
        "coef": lambda d: coarse_message(3, d, 1, 5),
        "rhs": lambda d: coarse_message(4, d, 0, 1),
        "post": post_message,
    }

    def each(name):
        return [d for d in range(8) if name != "post" or 0 in DIRS[d]]

    def send(name):
        for d in each(name):
            @pl.when(exists(*DIRS[d]))
            def _():
                kinds[name](d).start()

    def receive(name):
        for d in each(name):
            dx, dy = DIRS[d]
            @pl.when(exists(-dx, -dy))
            def _():
                kinds[name](d).wait_recv()

    def sent(name):
        for d in each(name):
            @pl.when(exists(*DIRS[d]))
            def _():
                kinds[name](d).wait_send()

    low_half = lax.broadcasted_iota(jnp.int32, (1, 8, 256), 1) < 4
    low_coarse = lax.broadcasted_iota(jnp.int32, (1, 8, 128), 1) < 4

    def turned(v):
        return pltpu.roll(v, 4, 1)

    def pair_up(a, b, low):
        return jnp.where(low, turned(b), a), jnp.where(low, a, turned(b))

    def pair_off(up, down, low):
        return jnp.where(low, down, up), turned(jnp.where(low, up, down))

    def pack(body, packed):
        for at, a, b, count in ((1, 3, 11, 8), (0, 3, 4, 1), (9, 17, 18, 1)):
            for way, lo in ((0, 8), (1, 0)):
                tiles = pair_up(body[a:a + count, lo:lo + 8], body[b:b + count, lo:lo + 8], low_half)
                packed[way, at:at + count] = tiles[way]

    for load, parts in zip(loads, ((ke, kpack), (pe, ppack), (se, spack))):
        load.wait()
        pack(*parts)
    pl.semaphore_wait(barrier, near_x * near_y - 1)
    send("k")
    send("p")
    send("s")

    def clear(ref, *index):
        view = ref.at[index]
        view[...] = jnp.zeros(view.shape, f32)

    for ref in (ke, pe):
        clear(ref, 0, slice(16, 24))
        clear(ref, 21, slice(16, 24))
    for dx, dy in DIRS:
        @pl.when(jnp.logical_not(exists(-dx, -dy)))
        def _():
            for ref, halo, wide in (
                (ke, khalo, 3), (pe, phalo, 3), (se, shalo, 2), (rr, None, 1),
            ):
                if dy == 0:
                    at = slice(3 - wide, 3) if dx > 0 else slice(19, 19 + wide)
                    clear(ref, at, slice(0, 16))
                else:
                    lo, hi = {0: (1, 9), 1: (0, 1), -1: (9, 10)}[dx]
                    if halo is not None:
                        clear(halo, FROM[dy] - 1, slice(lo, hi))
                    elif dx == 0:
                        clear(rhalo, FROM[dy] - 1)
            if dy == 0:
                clear({1: cl, -1: cr}[dx])
            else:
                clear({0: hm, 1: hl, -1: hr}[dx], FROM[dy] - 1)

    y_at = lax.broadcasted_iota(jnp.int32, (24, 256), 0)
    z_at = lax.broadcasted_iota(jnp.int32, (24, 256), 1)
    y_rel = jnp.where(y_at < 20, y_at, y_at - 24)
    y_glob = y_rel + row * width
    ends_yz = (
        (y_glob == 0).astype(f32) + (y_glob == rows * width - 1).astype(f32)
        + (z_at == 0).astype(f32) + (z_at == 255).astype(f32)
    )
    odd_y = (y_at & 1) == 1
    odd_z = (z_at & 1) == 1

    def loop(lo, hi, step, unroll=4):
        def run(i, carry):
            step(i)
            return carry
        lax.fori_loop(lo, hi, run, 0, unroll=unroll)

    def set_rim(body, halo):
        for at, a, b, count in ((1, 3, 11, 8), (0, 1, 2, 1), (9, 19, 20, 1)):
            here = slice(at, at + count)
            first, second = pair_off(halo[0, here], halo[1, here], low_half)
            body[a:a + count, 16:24] = first
            body[b:b + count, 16:24] = second

    def next_y(v):
        return pltpu.roll(v, 23, 0)

    def prev_y(v):
        return pltpu.roll(v, 1, 0)

    def next_z(v):
        return pltpu.roll(v, 255, 1)

    def prev_z(v):
        return pltpu.roll(v, 1, 1)

    def face(a, b):
        total = a + b
        return 2.0 * a * b / jnp.where(total > 0, total, 1.0)

    ids = [agg[slab * width + x] for x in range(width)]
    slots = [i - ids[0] for i in ids]
    live = slots[15]
    col = lax.broadcasted_iota(jnp.int32, (1, 256), 1)
    slot_col = jnp.zeros((1, 256), jnp.int32)
    for x in range(width):
        inside = (col >> 4) == x
        slot_col = jnp.where(inside, slots[x], slot_col)
    r168 = lax.broadcasted_iota(jnp.int32, (168, 256), 0)
    c168 = lax.broadcasted_iota(jnp.int32, (168, 256), 1)
    want = jnp.where(r168 < 128, r168 >> 3, (r168 >> 3) - 20 + live)
    gather = ((want == slot_col) & ((r168 & 7) == ((c168 & 15) >> 1))).astype(f32)
    gather = jnp.concatenate([gather, gather], axis=1).astype(jnp.bfloat16)
    zr = lax.broadcasted_iota(jnp.int32, (512, 128), 0)
    zc = lax.broadcasted_iota(jnp.int32, (512, 128), 1)
    pair_z = (((zr & 255) >> 1) == zc).astype(f32).astype(jnp.bfloat16)

    def coarsen(q0, q1):
        count = q1 - q0
        flat = fields[q0:q1].reshape(count * 256, 256)
        pairs = dot(jnp.concatenate(halves(flat), axis=1), pair_z)
        pairs = jnp.concatenate([pairs[256 * q:256 * (q + 1)] for q in range(count)], axis=1)
        sums = dot(gather, jnp.concatenate(halves(pairs), axis=0))
        for q in range(count):
            part = sums[:, 128 * q:128 * (q + 1)]
            cm[q0 + q] = part[0:128]
            cs[q0 + q] = part[128:168]

    def pack_coarse(packed, pair, a, b):
        tiles = pair_up(a.reshape(-1, 8, 128), b.reshape(-1, 8, 128), low_coarse)
        for way in range(2):
            packed[way, pair, 0:a.shape[0]] = tiles[way].reshape(a.shape)

    receive("k")
    set_rim(ke, khalo)

    def x_faces(i):
        fx[i] = face(ke[i], ke[i + 1])
    loop(0, 21, x_faces)

    def other_faces(i):
        k = ke[i]
        north = face(k, next_y(k))
        above = jnp.where(z_at == 255, 0.0, face(k, next_z(k)))
        south, below = prev_y(north), prev_z(above)
        x_glob = slab * width + i - 3
        ends_x = (x_glob == 0).astype(f32) + (x_glob == slabs * width - 1).astype(f32)
        bound = 2.0 * k * (ends_yz + ends_x)
        fy[i] = north
        fz[i] = above
        diag = fx[i - 1] + fx[i] + north + south + above + below + bound
        dg[i] = diag
        wt[i] = OMEGA / jnp.where(diag > 0, diag, 1.0)
        return north, above, south, below, bound

    def plain_faces(i):
        other_faces(i)

    def own_faces(i):
        north, above, south, below, bound = other_faces(i)
        x = slab * width + i - 3
        crossing = agg[x] != agg[jnp.minimum(x + 1, slabs * width - 1)]
        fields[1, i - 3] = fx[i, 0:16] * crossing.astype(f32)
        fields[2, i - 3] = jnp.where(odd_y, north, 0.0)[0:16]
        fields[3, i - 3] = jnp.where(odd_z, above, 0.0)[0:16]
        whole = bound + jnp.where(odd_y, north, south) + jnp.where(odd_z, above, below)
        fields[4, i - 3] = whole[0:16]

    loop(3, 19, own_faces)
    coarsen(1, 5)
    for pair, q in ((0, 1), (1, 3)):
        pack_coarse(cmp, pair, cm[q], cm[q + 1])
        pack_coarse(csp, pair, cs[q], cs[q + 1])
    send("coef")
    loop(1, 3, plain_faces)
    loop(19, 21, plain_faces)

    def beside(src, i):
        v = src[i]
        north, above = fy[i], fz[i]
        around = fx[i - 1] * src[i - 1] + fx[i] * src[i + 1]
        around = around + (north * next_y(v) + prev_y(north * v))
        return v, around + (above * next_z(v) + prev_z(above * v))

    def sweep(src, dst, lo, hi):
        def step(i):
            v, around = beside(src, i)
            dst[i] = (1.0 - OMEGA) * v + wt[i] * (se[i] + around)
        loop(lo, hi, step)

    receive("p")
    set_rim(pe, phalo)
    receive("s")
    set_rim(se, shalo)
    sweep(pe, p1, 1, 21)
    sweep(p1, p2, 2, 20)

    def residual(i):
        v, around = beside(p2, i)
        fields[0, i - 3] = (se[i] - dg[i] * v + around)[0:16]
    loop(3, 19, residual)
    coarsen(0, 1)
    pack_coarse(cmp, 2, cm[0, 0:64], cm[0, 64:128])
    send("rhs")

    rp = lax.broadcasted_iota(jnp.int32, (384, 64), 0)
    cp = lax.broadcasted_iota(jnp.int32, (384, 64), 1)
    place = (((rp >> 4) - (cp >> 4) == 4 + live) & ((rp & 15) == (cp & 15))).astype(f32)
    place = jnp.concatenate([place, place], axis=1).astype(jnp.bfloat16)

    def joined(part, halo, q, count):
        own = part[q].reshape(count, 8, 128)
        if q > 0:
            pair = (q - 1) // 2
            tiles = [halo[way, pair].reshape(count, 8, 128) for way in range(2)]
            rim = pair_off(*tiles, low_coarse)[(q - 1) % 2]
        elif count == 16:
            tiles = [halo[way, 2, 0:64].reshape(8, 8, 128) for way in range(2)]
            rim = jnp.concatenate(pair_off(*tiles, low_coarse), axis=0)
        else:
            tiles = [halo[way, 2].reshape(count, 8, 128) for way in range(2)]
            rim = pair_off(*tiles, low_coarse)[0]
        return jnp.concatenate([own, rim], axis=1)

    def extend(q0, q1):
        count = q1 - q0
        ahead = [joined(cr, hr, q, 4).reshape(64, 128) for q in range(q0, q1)]
        after = dot(place, jnp.concatenate(halves(jnp.concatenate(ahead, axis=1)), axis=0))
        for q in range(q0, q1):
            at = 128 * (q - q0)
            ext[q] = after[:, at:at + 128].reshape(24, 16, 128)
            ext[q, 0:5] += joined(cl, hl, q, 5)
            ext[q, 4:20] += joined(cm, hm, q, 16)

    receive("coef")
    extend(1, 5)
    zl = lax.broadcasted_iota(jnp.int32, (16, 128), 1)
    def diagonal(t):
        diag = ext[4, t] + ext[1, t] + ext[1, t - 1]
        corr[2, t] = OMEGA / jnp.where(diag > 0, diag, 1.0)
    loop(1, 23, diagonal)
    receive("rhs")
    extend(0, 1)

    def first(t):
        corr[0, t] = corr[2, t] * ext[0, t]
    loop(1, 23, first)
    for number, (lo, hi) in enumerate(((2, 22), (3, 21), (4, 20))):
        src, dst = number % 2, (number + 1) % 2
        def coarse_sweep(t):
            v = corr[src, t]
            north, above = ext[2, t], ext[3, t]
            around = ext[1, t] * corr[src, t + 1] + ext[1, t - 1] * corr[src, t - 1]
            around = around + (north * pltpu.roll(v, 15, 0) + pltpu.roll(north * v, 1, 0))
            around = around + (above * pltpu.roll(v, 127, 1) + pltpu.roll(above * v, 1, 1))
            corr[dst, t] = (1.0 - OMEGA) * v + corr[2, t] * (ext[0, t] + around)
        loop(lo, hi, coarse_sweep)

    ru = lax.broadcasted_iota(jnp.int32, (24, 256), 0)
    cu = lax.broadcasted_iota(jnp.int32, (24, 256), 1)
    same_y = (cu & 15) == jnp.where(ru < 20, ru >> 1, (ru >> 1) + 4)
    spread = jnp.concatenate(
        [(same_y & ((cu >> 4) == slots[x])).astype(f32) for x in range(width)], axis=0
    )
    er = lax.broadcasted_iota(jnp.int32, (256, 256), 0)
    ec = lax.broadcasted_iota(jnp.int32, (256, 256), 1)
    twice_z = ((ec >> 1) == (er & 127)).astype(f32).astype(jnp.bfloat16)
    coarse = jnp.concatenate(halves(corr[1, 4:20].reshape(256, 128)), axis=1)
    fine = dot(dot(spread.astype(jnp.bfloat16), coarse).astype(jnp.bfloat16), twice_z)
    fine = fine.reshape(16, 24, 256)
    p1[3:19] = p2[3:19] + fine
    p1[2] = p2[2] + fine[0]
    p1[19] = p2[19] + fine[15]
    sweep(p1, rr, 3, 19)
    edge[0] = rr[3:19, 15, :]
    edge[1] = rr[3:19, 0, :]
    send("post")
    receive("post")
    for i in range(16):
        rr[i + 3, 23:24] = rhalo[0, i:i + 1]
        rr[i + 3, 16:17] = rhalo[1, i:i + 1]

    def last(i):
        v, around = beside(rr, i)
        out[i - 3] = ((1.0 - OMEGA) * v + wt[i] * (se[i] + around))[0:16]
    loop(3, 19, last)
    for name in kinds:
        sent(name)


def store_kernel(field, out, sem):
    store = pltpu.make_async_copy(field, out, sem)
    store.start()
    store.wait()


def body(permeability, source, pressure, aggregate):
    f32 = jnp.float32
    shape = permeability.shape
    block = pltpu.VMEM((22, 24, 256), f32)
    halo = pltpu.VMEM((2, 10, 8, 256), f32)
    hbm = pl.BlockSpec(memory_space=pltpu.HBM)
    vmem = pl.BlockSpec(memory_space=pltpu.VMEM)
    result = pl.pallas_call(
        kernel,
        out_shape=jax.ShapeDtypeStruct(shape, f32),
        in_specs=[pl.BlockSpec(memory_space=pltpu.SMEM), hbm, hbm, hbm],
        out_specs=vmem,
        scratch_shapes=[block, block, block, halo, halo, halo]
        + [block] * 8
        + [
            pltpu.VMEM((2, 16, 256), f32),
            halo,
            halo,
            halo,
            pltpu.VMEM((2, 16, 256), f32),
            pltpu.VMEM((5, 16, 16, 256), f32),
            pltpu.VMEM((5, 128, 128), f32),
            pltpu.VMEM((5, 40, 128), f32),
            pltpu.VMEM((5, 32, 128), f32),
            pltpu.VMEM((5, 40, 128), f32),
            pltpu.VMEM((2, 3, 128, 128), f32),
            pltpu.VMEM((2, 2, 40, 128), f32),
            pltpu.VMEM((2, 3, 128, 128), f32),
            pltpu.VMEM((2, 3, 40, 128), f32),
            pltpu.VMEM((2, 3, 32, 128), f32),
            pltpu.VMEM((5, 24, 16, 128), f32),
            pltpu.VMEM((3, 24, 16, 128), f32),
            pltpu.SemaphoreType.DMA((3,)),
            pltpu.SemaphoreType.DMA((48,)),
            pltpu.SemaphoreType.DMA((48,)),
        ],
        compiler_params=pltpu.CompilerParams(
            collective_id=0, has_side_effects=True, vmem_limit_bytes=GRANT
        ),
    )(aggregate, permeability, source, pressure)
    return pl.pallas_call(
        store_kernel,
        out_shape=jax.ShapeDtypeStruct(shape, f32),
        in_specs=[vmem],
        out_specs=hbm,
        scratch_shapes=[pltpu.SemaphoreType.DMA],
    )(result)


def solution(mesh):
    spec = P(("real", "slab"), ("pencil", "sub"), None)
    return jax.shard_map(
        body, mesh=mesh, in_specs=(spec, spec, spec, P("real")), out_specs=spec, check_vma=False
    )
```

```python
import functools
import jax
import jax.numpy as jnp
from jax import lax
from jax.experimental import pallas as pl
from jax.experimental.pallas import tpu as pltpu
from jax.sharding import PartitionSpec as P

OMEGA = 0.8
GRANT = 62 * 2**20
MESH = pl.DeviceIdType.MESH

DIRS = [(dx, dy) for dx in (1, 0, -1) for dy in (1, 0, -1) if (dx, dy) != (0, 0)]
FROM = {0: 0, 1: 1, -1: 2}


def dot(a, b):
    return jnp.dot(a, b, preferred_element_type=jnp.float32)


def halves(v):
    upper = v.astype(jnp.bfloat16)
    return upper, (v - upper.astype(jnp.float32)).astype(jnp.bfloat16)


def kernel(
    agg, k_in, s_in, p_in, out,
    ke, se, pe, khalo, shalo, phalo, fx, fy, fz, dg, wt, p1, p2, rr, rhalo,
    kpack, ppack, spack, edge, xhalo, result, fields, cm, cl, cr, cs, cmp, csp, hm, hl, hr, ext, corr, local_sem, send_sem, recv_sem,
):
    f32 = jnp.float32
    width = 16
    slab, slabs = lax.axis_index("slab"), lax.axis_size("slab")
    subs = lax.axis_size("sub")
    rows = lax.axis_size("pencil") * subs
    row = lax.axis_index("pencil") * subs + lax.axis_index("sub")

    loads = [
        pltpu.make_async_copy(src, dst.at[3:19, 0:16], local_sem.at[i])
        for i, (src, dst) in enumerate(((k_in, ke), (p_in, pe), (s_in, se)))
    ]
    for load in loads:
        load.start()

    def exists(dx, dy):
        ok = None
        for pos, step, count in ((slab, dx, slabs), (row, dy, rows)):
            if step:
                here = (pos + step < count) if step > 0 else (pos > 0)
                ok = here if ok is None else jnp.logical_and(ok, here)
        return ok

    def device(dx, dy):
        r = row + dy
        return {"slab": slab + dx, "pencil": r // subs, "sub": r % subs}

    barrier = pltpu.get_barrier_semaphore()
    for dx, dy in DIRS:
        @pl.when(exists(dx, dy))
        def _():
            pl.semaphore_signal(barrier, inc=1, device_id=device(dx, dy), device_id_type=MESH)
    near_x = 1 + (slab > 0).astype(jnp.int32) + (slab < slabs - 1).astype(jnp.int32)
    near_y = 1 + (row > 0).astype(jnp.int32) + (row < rows - 1).astype(jnp.int32)

    def message(kind, d, src, dst):
        return pltpu.make_async_remote_copy(
            src_ref=src, dst_ref=dst,
            send_sem=send_sem.at[kind * 8 + d], recv_sem=recv_sem.at[kind * 8 + d],
            device_id=device(*DIRS[d]), device_id_type=MESH,
        )

    def fine_message(kind, d, body, packed, halo, wide):
        dx, dy = DIRS[d]
        if dy == 0:
            src0 = 19 - wide if dx > 0 else 3
            dst0 = 3 - wide if dx > 0 else 19
            return message(kind, d, body.at[src0:src0 + wide, 0:16], body.at[dst0:dst0 + wide, 0:16])
        src0, dst0, length = {0: (1, 1, 8), 1: (9, 0, 1), -1: (0, 9, 1)}[dx]
        return message(
            kind, d, packed.at[FROM[dy] - 1, src0:src0 + length],
            halo.at[FROM[dy] - 1, dst0:dst0 + length],
        )

    def coarse_message(kind, d, q0, q1):
        dx, dy = DIRS[d]
        if dy == 0:
            qs = pl.ds(q0, q1 - q0)
            if dx > 0:
                return message(kind, d, cs.at[qs], cl.at[qs])
            return message(kind, d, cm.at[qs, 0:32], cr.at[qs])
        here = FROM[dy] - 1
        if q0 == 0:
            if dx > 0:
                return message(kind, d, cs.at[0], hl.at[here, 2])
            if dx < 0:
                return message(kind, d, cm.at[0, 0:32], hr.at[here, 2])
            return message(kind, d, cmp.at[here, 2, 0:64], hm.at[here, 2, 0:64])
        if dx > 0:
            return message(kind, d, csp.at[here], hl.at[here, 0:2])
        if dx < 0:
            return message(kind, d, cmp.at[here, 0:2, 0:32], hr.at[here, 0:2])
        return message(kind, d, cmp.at[here, 0:2], hm.at[here, 0:2])

    def post_message(d):
        dx, dy = DIRS[d]
        if dx > 0:
            return message(5, d, rr.at[18, 0:16], xhalo.at[0])
        if dx < 0:
            return message(5, d, rr.at[3, 0:16], xhalo.at[1])
        return message(5, d, edge.at[FROM[dy] - 1], rhalo.at[FROM[dy] - 1])

    kinds = {
        "k": lambda d: fine_message(0, d, ke, kpack, khalo, 3),
        "p": lambda d: fine_message(1, d, pe, ppack, phalo, 3),
        "s": lambda d: fine_message(2, d, se, spack, shalo, 2),
        "coef": lambda d: coarse_message(3, d, 1, 5),
        "rhs": lambda d: coarse_message(4, d, 0, 1),
        "post": post_message,
    }

    def each(name):
        return [d for d in range(8) if name != "post" or 0 in DIRS[d]]

    def send(name):
        for d in each(name):
            @pl.when(exists(*DIRS[d]))
            def _():
                kinds[name](d).start()

    def receive(name):
        for d in each(name):
            dx, dy = DIRS[d]
            @pl.when(exists(-dx, -dy))
            def _():
                kinds[name](d).wait_recv()

    def sent(name):
        for d in each(name):
            @pl.when(exists(*DIRS[d]))
            def _():
                kinds[name](d).wait_send()

    low_half = lax.broadcasted_iota(jnp.int32, (1, 8, 256), 1) < 4
    low_coarse = lax.broadcasted_iota(jnp.int32, (1, 8, 128), 1) < 4

    def turned(v):
        return pltpu.roll(v, 4, 1)

    def pair_up(a, b, low):
        return jnp.where(low, turned(b), a), jnp.where(low, a, turned(b))

    def pair_off(up, down, low):
        return jnp.where(low, down, up), turned(jnp.where(low, up, down))

    def pack(body, packed):
        for at, a, b, count in ((1, 3, 11, 8), (0, 3, 4, 1), (9, 17, 18, 1)):
            for way, lo in ((0, 8), (1, 0)):
                tiles = pair_up(body[a:a + count, lo:lo + 8], body[b:b + count, lo:lo + 8], low_half)
                packed[way, at:at + count] = tiles[way]

    for name, load, parts in zip("kps", loads, ((ke, kpack), (pe, ppack), (se, spack))):
        load.wait()
        pack(*parts)
        if name == "k":
            pl.semaphore_wait(barrier, near_x * near_y - 1)
        send(name)

    def clear(ref, *index):
        view = ref.at[index]
        view[...] = jnp.zeros(view.shape, f32)

    for ref in (ke, pe):
        clear(ref, 0, slice(16, 24))
        clear(ref, 21, slice(16, 24))
    clear(rr, 2)
    clear(rr, 19)
    for dx, dy in DIRS:
        @pl.when(jnp.logical_not(exists(-dx, -dy)))
        def _():
            if dx == 0:
                clear(rhalo, FROM[dy] - 1)
            if dy == 0:
                clear(xhalo, 0 if dx > 0 else 1)
            for ref, halo, wide in ((ke, khalo, 3), (pe, phalo, 3), (se, shalo, 2)):
                if dy == 0:
                    at = slice(3 - wide, 3) if dx > 0 else slice(19, 19 + wide)
                    clear(ref, at, slice(0, 16))
                else:
                    lo, hi = {0: (1, 9), 1: (0, 1), -1: (9, 10)}[dx]
                    clear(halo, FROM[dy] - 1, slice(lo, hi))
            if dy == 0:
                clear({1: cl, -1: cr}[dx])
            else:
                clear({0: hm, 1: hl, -1: hr}[dx], FROM[dy] - 1)

    y_at = lax.broadcasted_iota(jnp.int32, (24, 256), 0)
    z_at = lax.broadcasted_iota(jnp.int32, (24, 256), 1)
    y_rel = jnp.where(y_at < 20, y_at, y_at - 24)
    y_glob = y_rel + row * width
    ends_yz = (
        (y_glob == 0).astype(f32) + (y_glob == rows * width - 1).astype(f32)
        + (z_at == 0).astype(f32) + (z_at == 255).astype(f32)
    )
    odd_y = (y_at & 1) == 1
    odd_z = (z_at & 1) == 1

    def loop(lo, hi, step, unroll=4):
        def run(i, carry):
            step(i)
            return carry
        lax.fori_loop(lo, hi, run, 0, unroll=unroll)

    def set_rim(body, halo):
        for at, a, b, count in ((1, 3, 11, 8), (0, 1, 2, 1), (9, 19, 20, 1)):
            here = slice(at, at + count)
            first, second = pair_off(halo[0, here], halo[1, here], low_half)
            body[a:a + count, 16:24] = first
            body[b:b + count, 16:24] = second

    def next_y(v):
        return pltpu.roll(v, 23, 0)

    def prev_y(v):
        return pltpu.roll(v, 1, 0)

    def next_z(v):
        return pltpu.roll(v, 255, 1)

    def prev_z(v):
        return pltpu.roll(v, 1, 1)

    def face(a, b):
        total = a + b
        return 2.0 * a * b / jnp.where(total > 0, total, 1.0)

    ids = [agg[slab * width + x] for x in range(width)]
    slots = [i - ids[0] for i in ids]
    live = slots[15]
    col = lax.broadcasted_iota(jnp.int32, (1, 256), 1)
    slot_col = jnp.zeros((1, 256), jnp.int32)
    for x in range(width):
        inside = (col >> 4) == x
        slot_col = jnp.where(inside, slots[x], slot_col)
    r168 = lax.broadcasted_iota(jnp.int32, (168, 256), 0)
    c168 = lax.broadcasted_iota(jnp.int32, (168, 256), 1)
    want = jnp.where(r168 < 128, r168 >> 3, (r168 >> 3) - 20 + live)
    gather = ((want == slot_col) & ((r168 & 7) == ((c168 & 15) >> 1))).astype(f32)
    gather = jnp.concatenate([gather, gather], axis=1).astype(jnp.bfloat16)
    zr = lax.broadcasted_iota(jnp.int32, (512, 128), 0)
    zc = lax.broadcasted_iota(jnp.int32, (512, 128), 1)
    pair_z = (((zr & 255) >> 1) == zc).astype(f32).astype(jnp.bfloat16)

    def coarsen(q0, q1):
        count = q1 - q0
        flat = fields[q0:q1].reshape(count * 256, 256)
        pairs = dot(jnp.concatenate(halves(flat), axis=1), pair_z)
        pairs = jnp.concatenate([pairs[256 * q:256 * (q + 1)] for q in range(count)], axis=1)
        sums = dot(gather, jnp.concatenate(halves(pairs), axis=0))
        for q in range(count):
            part = sums[:, 128 * q:128 * (q + 1)]
            cm[q0 + q] = part[0:128]
            cs[q0 + q] = part[128:168]

    def pack_coarse(packed, pair, a, b):
        tiles = pair_up(a.reshape(-1, 8, 128), b.reshape(-1, 8, 128), low_coarse)
        for way in range(2):
            packed[way, pair, 0:a.shape[0]] = tiles[way].reshape(a.shape)

    receive("k")
    set_rim(ke, khalo)

    def x_faces(i):
        fx[i] = face(ke[i], ke[i + 1])
    loop(0, 21, x_faces)

    def other_faces(i):
        k = ke[i]
        north = face(k, next_y(k))
        above = jnp.where(z_at == 255, 0.0, face(k, next_z(k)))
        south, below = prev_y(north), prev_z(above)
        x_glob = slab * width + i - 3
        ends_x = (x_glob == 0).astype(f32) + (x_glob == slabs * width - 1).astype(f32)
        bound = 2.0 * k * (ends_yz + ends_x)
        fy[i] = north
        fz[i] = above
        diag = fx[i - 1] + fx[i] + north + south + above + below + bound
        dg[i] = diag
        wt[i] = OMEGA / jnp.where(diag > 0, diag, 1.0)
        return north, above, south, below, bound

    def plain_faces(i):
        other_faces(i)

    def own_faces(i):
        north, above, south, below, bound = other_faces(i)
        x = slab * width + i - 3
        crossing = agg[x] != agg[jnp.minimum(x + 1, slabs * width - 1)]
        fields[1, i - 3] = fx[i, 0:16] * crossing.astype(f32)
        fields[2, i - 3] = jnp.where(odd_y, north, 0.0)[0:16]
        fields[3, i - 3] = jnp.where(odd_z, above, 0.0)[0:16]
        whole = bound + jnp.where(odd_y, north, south) + jnp.where(odd_z, above, below)
        fields[4, i - 3] = whole[0:16]

    loop(3, 19, own_faces)
    coarsen(1, 5)
    for pair, q in ((0, 1), (1, 3)):
        pack_coarse(cmp, pair, cm[q], cm[q + 1])
        pack_coarse(csp, pair, cs[q], cs[q + 1])
    send("coef")
    loop(1, 3, plain_faces)
    loop(19, 21, plain_faces)

    def beside(src, i):
        v = src[i]
        north, above = fy[i], fz[i]
        around = fx[i - 1] * src[i - 1] + fx[i] * src[i + 1]
        around = around + (north * next_y(v) + prev_y(north * v))
        return v, around + (above * next_z(v) + prev_z(above * v))

    def sweep(src, dst, lo, hi):
        def step(i):
            v, around = beside(src, i)
            dst[i] = (1.0 - OMEGA) * v + wt[i] * (se[i] + around)
        loop(lo, hi, step)

    receive("p")
    set_rim(pe, phalo)
    receive("s")
    set_rim(se, shalo)
    sweep(pe, p1, 1, 21)
    sweep(p1, p2, 2, 20)

    def residual(i):
        v, around = beside(p2, i)
        fields[0, i - 3] = (se[i] - dg[i] * v + around)[0:16]
    loop(3, 19, residual)
    coarsen(0, 1)
    pack_coarse(cmp, 2, cm[0, 0:64], cm[0, 64:128])
    send("rhs")

    rp = lax.broadcasted_iota(jnp.int32, (384, 64), 0)
    cp = lax.broadcasted_iota(jnp.int32, (384, 64), 1)
    place = (((rp >> 4) - (cp >> 4) == 4 + live) & ((rp & 15) == (cp & 15))).astype(f32)
    place = jnp.concatenate([place, place], axis=1).astype(jnp.bfloat16)

    def joined(part, halo, q, count):
        own = part[q].reshape(count, 8, 128)
        if q > 0:
            pair = (q - 1) // 2
            tiles = [halo[way, pair].reshape(count, 8, 128) for way in range(2)]
            rim = pair_off(*tiles, low_coarse)[(q - 1) % 2]
        elif count == 16:
            tiles = [halo[way, 2, 0:64].reshape(8, 8, 128) for way in range(2)]
            rim = jnp.concatenate(pair_off(*tiles, low_coarse), axis=0)
        else:
            tiles = [halo[way, 2].reshape(count, 8, 128) for way in range(2)]
            rim = pair_off(*tiles, low_coarse)[0]
        return jnp.concatenate([own, rim], axis=1)

    def extend(q0, q1):
        count = q1 - q0
        ahead = [joined(cr, hr, q, 4).reshape(64, 128) for q in range(q0, q1)]
        after = dot(place, jnp.concatenate(halves(jnp.concatenate(ahead, axis=1)), axis=0))
        for q in range(q0, q1):
            at = 128 * (q - q0)
            ext[q] = after[:, at:at + 128].reshape(24, 16, 128)
            ext[q, 0:5] += joined(cl, hl, q, 5)
            ext[q, 4:20] += joined(cm, hm, q, 16)

    receive("coef")
    extend(1, 5)
    zl = lax.broadcasted_iota(jnp.int32, (16, 128), 1)
    def diagonal(t):
        diag = ext[4, t] + ext[1, t] + ext[1, t - 1]
        corr[2, t] = OMEGA / jnp.where(diag > 0, diag, 1.0)
    loop(1, 23, diagonal)
    ru = lax.broadcasted_iota(jnp.int32, (24, 256), 0)
    cu = lax.broadcasted_iota(jnp.int32, (24, 256), 1)
    same_y = (cu & 15) == jnp.where(ru < 20, ru >> 1, (ru >> 1) + 4)
    spread = jnp.concatenate(
        [(same_y & ((cu >> 4) == slots[x])).astype(f32) for x in range(width)], axis=0
    )
    er = lax.broadcasted_iota(jnp.int32, (256, 256), 0)
    ec = lax.broadcasted_iota(jnp.int32, (256, 256), 1)
    twice_z = ((ec >> 1) == (er & 127)).astype(f32).astype(jnp.bfloat16)
    receive("rhs")
    extend(0, 1)

    def first(t):
        corr[0, t] = corr[2, t] * ext[0, t]
    loop(1, 23, first)
    for number, (lo, hi) in enumerate(((2, 22), (3, 21), (4, 20))):
        src, dst = number % 2, (number + 1) % 2
        def coarse_sweep(t):
            v = corr[src, t]
            north, above = ext[2, t], ext[3, t]
            around = ext[1, t] * corr[src, t + 1] + ext[1, t - 1] * corr[src, t - 1]
            around = around + (north * pltpu.roll(v, 15, 0) + pltpu.roll(north * v, 1, 0))
            around = around + (above * pltpu.roll(v, 127, 1) + pltpu.roll(above * v, 1, 1))
            corr[dst, t] = (1.0 - OMEGA) * v + corr[2, t] * (ext[0, t] + around)
        loop(lo, hi, coarse_sweep)

    coarse = jnp.concatenate(halves(corr[1, 4:20].reshape(256, 128)), axis=1)
    fine = dot(dot(spread.astype(jnp.bfloat16), coarse).astype(jnp.bfloat16), twice_z)
    fine = fine.reshape(16, 24, 256)
    p1[3:19] = p2[3:19] + fine
    p1[2] = p2[2] + fine[0]
    p1[19] = p2[19] + fine[15]
    sweep(p1, rr, 3, 19)
    edge[0] = rr[3:19, 15, :]
    edge[1] = rr[3:19, 0, :]
    send("post")
    clear(rr, slice(3, 19), slice(16, 24))

    def last(i):
        v, around = beside(rr, i)
        result[i - 3] = ((1.0 - OMEGA) * v + wt[i] * (se[i] + around))[0:16]
    loop(3, 19, last)
    south = wt[3:19, 0, :] * fy[3:19, 23, :]
    north = wt[3:19, 15, :] * fy[3:19, 15, :]
    receive("post")
    result[0] += (wt[3, 0:16] * fx[2, 0:16]) * xhalo[0]
    result[15] += (wt[18, 0:16] * fx[18, 0:16]) * xhalo[1]
    result[:, 0, :] = result[:, 0, :] + south * rhalo[0]
    result[:, 15, :] = result[:, 15, :] + north * rhalo[1]
    store = pltpu.make_async_copy(result, out, local_sem.at[0])
    store.start()
    for name in kinds:
        sent(name)
    store.wait()


def body(permeability, source, pressure, aggregate):
    f32 = jnp.float32
    shape = permeability.shape
    block = pltpu.VMEM((22, 24, 256), f32)
    halo = pltpu.VMEM((2, 10, 8, 256), f32)
    hbm = pl.BlockSpec(memory_space=pltpu.HBM)
    return pl.pallas_call(
        kernel,
        out_shape=jax.ShapeDtypeStruct(shape, f32),
        in_specs=[pl.BlockSpec(memory_space=pltpu.SMEM), hbm, hbm, hbm],
        out_specs=hbm,
        scratch_shapes=[block, block, block, halo, halo, halo]
        + [block] * 8
        + [
            pltpu.VMEM((2, 16, 256), f32),
            halo,
            halo,
            halo,
            pltpu.VMEM((2, 16, 256), f32),
            pltpu.VMEM((2, 16, 256), f32),
            pltpu.VMEM((16, 16, 256), f32),
            pltpu.VMEM((5, 16, 16, 256), f32),
            pltpu.VMEM((5, 128, 128), f32),
            pltpu.VMEM((5, 40, 128), f32),
            pltpu.VMEM((5, 32, 128), f32),
            pltpu.VMEM((5, 40, 128), f32),
            pltpu.VMEM((2, 3, 128, 128), f32),
            pltpu.VMEM((2, 2, 40, 128), f32),
            pltpu.VMEM((2, 3, 128, 128), f32),
            pltpu.VMEM((2, 3, 40, 128), f32),
            pltpu.VMEM((2, 3, 32, 128), f32),
            pltpu.VMEM((5, 24, 16, 128), f32),
            pltpu.VMEM((3, 24, 16, 128), f32),
            pltpu.SemaphoreType.DMA((3,)),
            pltpu.SemaphoreType.DMA((48,)),
            pltpu.SemaphoreType.DMA((48,)),
        ],
        compiler_params=pltpu.CompilerParams(
            collective_id=0, has_side_effects=True, vmem_limit_bytes=GRANT
        ),
    )(aggregate, permeability, source, pressure)

def solution(mesh):
    spec = P(("real", "slab"), ("pencil", "sub"), None)
    return jax.shard_map(
        body, mesh=mesh, in_specs=(spec, spec, spec, P("real")), out_specs=spec, check_vma=False
    )
```

```python
import functools
import jax
import jax.numpy as jnp
from jax import lax
from jax.experimental import pallas as pl
from jax.experimental.pallas import tpu as pltpu
from jax.sharding import PartitionSpec as P

OMEGA = 0.8
GRANT = 62 * 2**20
MESH = pl.DeviceIdType.MESH

DIRS = [(dx, dy) for dx in (1, 0, -1) for dy in (1, 0, -1) if (dx, dy) != (0, 0)]
FROM = {0: 0, 1: 1, -1: 2}


def dot(a, b):
    return jnp.dot(a, b, preferred_element_type=jnp.float32)


def halves(v):
    upper = v.astype(jnp.bfloat16)
    return upper, (v - upper.astype(jnp.float32)).astype(jnp.bfloat16)


def kernel(
    agg, k_in, s_in, p_in, out,
    ke, se, pe, khalo, shalo, phalo, fx, fy, fz, dg, wt, p1, p2, rr, rhalo,
    kpack, ppack, spack, edge, xhalo, result, fields, cm, cl, cr, cs, cmp, csp, hm, hl, hr, ext, corr, local_sem, send_sem, recv_sem,
):
    f32 = jnp.float32
    width = 16
    slab, slabs = lax.axis_index("slab"), lax.axis_size("slab")
    subs = lax.axis_size("sub")
    rows = lax.axis_size("pencil") * subs
    row = lax.axis_index("pencil") * subs + lax.axis_index("sub")

    loads = [
        pltpu.make_async_copy(src, dst.at[3:19, 0:16], local_sem.at[i])
        for i, (src, dst) in enumerate(((k_in, ke), (p_in, pe), (s_in, se)))
    ]
    for load in loads:
        load.start()

    def exists(dx, dy):
        ok = None
        for pos, step, count in ((slab, dx, slabs), (row, dy, rows)):
            if step:
                here = (pos + step < count) if step > 0 else (pos > 0)
                ok = here if ok is None else jnp.logical_and(ok, here)
        return ok

    def device(dx, dy):
        r = row + dy
        return {"slab": slab + dx, "pencil": r // subs, "sub": r % subs}

    barrier = pltpu.get_barrier_semaphore()
    for dx, dy in DIRS:
        @pl.when(exists(dx, dy))
        def _():
            pl.semaphore_signal(barrier, inc=1, device_id=device(dx, dy), device_id_type=MESH)
    near_x = 1 + (slab > 0).astype(jnp.int32) + (slab < slabs - 1).astype(jnp.int32)
    near_y = 1 + (row > 0).astype(jnp.int32) + (row < rows - 1).astype(jnp.int32)

    def message(kind, d, src, dst):
        return pltpu.make_async_remote_copy(
            src_ref=src, dst_ref=dst,
            send_sem=send_sem.at[kind * 8 + d], recv_sem=recv_sem.at[kind * 8 + d],
            device_id=device(*DIRS[d]), device_id_type=MESH,
        )

    def fine_message(kind, d, body, packed, halo, wide):
        dx, dy = DIRS[d]
        if dy == 0:
            src0 = 19 - wide if dx > 0 else 3
            dst0 = 3 - wide if dx > 0 else 19
            return message(kind, d, body.at[src0:src0 + wide, 0:16], body.at[dst0:dst0 + wide, 0:16])
        src0, dst0, length = {0: (1, 1, 8), 1: (9, 0, 1), -1: (0, 9, 1)}[dx]
        return message(
            kind, d, packed.at[FROM[dy] - 1, src0:src0 + length],
            halo.at[FROM[dy] - 1, dst0:dst0 + length],
        )

    def coarse_message(kind, d, q0, q1):
        dx, dy = DIRS[d]
        if dy == 0:
            qs = pl.ds(q0, q1 - q0)
            if dx > 0:
                return message(kind, d, cs.at[qs], cl.at[qs])
            return message(kind, d, cm.at[qs, 0:32], cr.at[qs])
        here = FROM[dy] - 1
        if q0 == 0:
            if dx > 0:
                return message(kind, d, cs.at[0], hl.at[here, 2])
            if dx < 0:
                return message(kind, d, cm.at[0, 0:32], hr.at[here, 2])
            return message(kind, d, cmp.at[here, 2, 0:64], hm.at[here, 2, 0:64])
        if dx > 0:
            return message(kind, d, csp.at[here], hl.at[here, 0:2])
        if dx < 0:
            return message(kind, d, cmp.at[here, 0:2, 0:32], hr.at[here, 0:2])
        return message(kind, d, cmp.at[here, 0:2], hm.at[here, 0:2])

    def post_message(d):
        dx, dy = DIRS[d]
        if dx > 0:
            return message(5, d, rr.at[18, 0:16], xhalo.at[0])
        if dx < 0:
            return message(5, d, rr.at[3, 0:16], xhalo.at[1])
        return message(5, d, edge.at[FROM[dy] - 1], rhalo.at[FROM[dy] - 1])

    kinds = {
        "k": lambda d: fine_message(0, d, ke, kpack, khalo, 3),
        "p": lambda d: fine_message(1, d, pe, ppack, phalo, 3),
        "s": lambda d: fine_message(2, d, se, spack, shalo, 2),
        "coef": lambda d: coarse_message(3, d, 1, 5),
        "rhs": lambda d: coarse_message(4, d, 0, 1),
        "post": post_message,
    }

    def each(name):
        return [d for d in range(8) if name != "post" or 0 in DIRS[d]]

    def send(name):
        for d in each(name):
            @pl.when(exists(*DIRS[d]))
            def _():
                kinds[name](d).start()

    def receive(name):
        for d in each(name):
            dx, dy = DIRS[d]
            @pl.when(exists(-dx, -dy))
            def _():
                kinds[name](d).wait_recv()

    def sent(name):
        for d in each(name):
            @pl.when(exists(*DIRS[d]))
            def _():
                kinds[name](d).wait_send()

    low_half = lax.broadcasted_iota(jnp.int32, (1, 8, 256), 1) < 4
    low_coarse = lax.broadcasted_iota(jnp.int32, (1, 8, 128), 1) < 4

    def turned(v):
        return pltpu.roll(v, 4, 1)

    def pair_up(a, b, low):
        return jnp.where(low, turned(b), a), jnp.where(low, a, turned(b))

    def pair_off(up, down, low):
        return jnp.where(low, down, up), turned(jnp.where(low, up, down))

    def pack(body, packed):
        for at, a, b, count in ((1, 3, 11, 8), (0, 3, 4, 1), (9, 17, 18, 1)):
            for way, lo in ((0, 8), (1, 0)):
                tiles = pair_up(body[a:a + count, lo:lo + 8], body[b:b + count, lo:lo + 8], low_half)
                packed[way, at:at + count] = tiles[way]

    for name, load, parts in zip("kps", loads, ((ke, kpack), (pe, ppack), (se, spack))):
        load.wait()
        pack(*parts)
        if name == "k":
            pl.semaphore_wait(barrier, near_x * near_y - 1)
        send(name)

    def clear(ref, *index):
        view = ref.at[index]
        view[...] = jnp.zeros(view.shape, f32)

    for ref in (ke, pe):
        clear(ref, 0, slice(16, 24))
        clear(ref, 21, slice(16, 24))
    clear(rr, 2)
    clear(rr, 19)
    for dx, dy in DIRS:
        @pl.when(jnp.logical_not(exists(-dx, -dy)))
        def _():
            if dx == 0:
                clear(rhalo, FROM[dy] - 1)
            if dy == 0:
                clear(xhalo, 0 if dx > 0 else 1)
            for ref, halo, wide in ((ke, khalo, 3), (pe, phalo, 3), (se, shalo, 2)):
                if dy == 0:
                    at = slice(3 - wide, 3) if dx > 0 else slice(19, 19 + wide)
                    clear(ref, at, slice(0, 16))
                else:
                    lo, hi = {0: (1, 9), 1: (0, 1), -1: (9, 10)}[dx]
                    clear(halo, FROM[dy] - 1, slice(lo, hi))
            if dy == 0:
                clear({1: cl, -1: cr}[dx])
            else:
                clear({0: hm, 1: hl, -1: hr}[dx], FROM[dy] - 1)

    y_at = lax.broadcasted_iota(jnp.int32, (24, 256), 0)
    z_at = lax.broadcasted_iota(jnp.int32, (24, 256), 1)
    y_rel = jnp.where(y_at < 20, y_at, y_at - 24)
    y_glob = y_rel + row * width
    ends_yz = (
        (y_glob == 0).astype(f32) + (y_glob == rows * width - 1).astype(f32)
        + (z_at == 0).astype(f32) + (z_at == 255).astype(f32)
    )
    odd_y = (y_at & 1) == 1
    odd_z = (z_at & 1) == 1

    def loop(lo, hi, step, whole=False):
        count = hi - lo
        unroll = count if whole else next(u for u in (10, 8, 7, 6, 2, 1) if count % u == 0)

        def run(i, carry):
            step(i)
            return carry
        lax.fori_loop(lo, hi, run, 0, unroll=unroll)

    def set_rim(body, halo):
        for at, a, b, count in ((1, 3, 11, 8), (0, 1, 2, 1), (9, 19, 20, 1)):
            here = slice(at, at + count)
            first, second = pair_off(halo[0, here], halo[1, here], low_half)
            body[a:a + count, 16:24] = first
            body[b:b + count, 16:24] = second

    def next_y(v):
        return pltpu.roll(v, 23, 0)

    def prev_y(v):
        return pltpu.roll(v, 1, 0)

    def next_z(v):
        return pltpu.roll(v, 255, 1)

    def prev_z(v):
        return pltpu.roll(v, 1, 1)

    def face(a, b):
        total = a + b
        return 2.0 * a * b / jnp.where(total > 0, total, 1.0)

    ids = [agg[slab * width + x] for x in range(width)]
    slots = [i - ids[0] for i in ids]
    live = slots[15]
    col = lax.broadcasted_iota(jnp.int32, (1, 256), 1)
    slot_col = jnp.zeros((1, 256), jnp.int32)
    for x in range(width):
        inside = (col >> 4) == x
        slot_col = jnp.where(inside, slots[x], slot_col)
    r168 = lax.broadcasted_iota(jnp.int32, (168, 256), 0)
    c168 = lax.broadcasted_iota(jnp.int32, (168, 256), 1)
    want = jnp.where(r168 < 128, r168 >> 3, (r168 >> 3) - 20 + live)
    gather = ((want == slot_col) & ((r168 & 7) == ((c168 & 15) >> 1))).astype(f32)
    gather = jnp.concatenate([gather, gather], axis=1).astype(jnp.bfloat16)
    zr = lax.broadcasted_iota(jnp.int32, (512, 128), 0)
    zc = lax.broadcasted_iota(jnp.int32, (512, 128), 1)
    pair_z = (((zr & 255) >> 1) == zc).astype(f32).astype(jnp.bfloat16)

    def coarsen(q0, q1):
        count = q1 - q0
        flat = fields[q0:q1].reshape(count * 256, 256)
        pairs = dot(jnp.concatenate(halves(flat), axis=1), pair_z)
        pairs = jnp.concatenate([pairs[256 * q:256 * (q + 1)] for q in range(count)], axis=1)
        sums = dot(gather, jnp.concatenate(halves(pairs), axis=0))
        for q in range(count):
            part = sums[:, 128 * q:128 * (q + 1)]
            cm[q0 + q] = part[0:128]
            cs[q0 + q] = part[128:168]

    def pack_coarse(packed, pair, a, b):
        tiles = pair_up(a.reshape(-1, 8, 128), b.reshape(-1, 8, 128), low_coarse)
        for way in range(2):
            packed[way, pair, 0:a.shape[0]] = tiles[way].reshape(a.shape)

    receive("k")
    set_rim(ke, khalo)

    def x_faces(i):
        fx[i] = face(ke[i], ke[i + 1])
    loop(0, 21, x_faces)

    def other_faces(i):
        k = ke[i]
        north = face(k, next_y(k))
        above = jnp.where(z_at == 255, 0.0, face(k, next_z(k)))
        south, below = prev_y(north), prev_z(above)
        x_glob = slab * width + i - 3
        ends_x = (x_glob == 0).astype(f32) + (x_glob == slabs * width - 1).astype(f32)
        bound = 2.0 * k * (ends_yz + ends_x)
        fy[i] = north
        fz[i] = above
        diag = fx[i - 1] + fx[i] + north + south + above + below + bound
        dg[i] = diag
        wt[i] = OMEGA / jnp.where(diag > 0, diag, 1.0)
        return north, above, south, below, bound

    def plain_faces(i):
        other_faces(i)

    def own_faces(i):
        north, above, south, below, bound = other_faces(i)
        x = slab * width + i - 3
        crossing = agg[x] != agg[jnp.minimum(x + 1, slabs * width - 1)]
        fields[1, i - 3] = fx[i, 0:16] * crossing.astype(f32)
        fields[2, i - 3] = jnp.where(odd_y, north, 0.0)[0:16]
        fields[3, i - 3] = jnp.where(odd_z, above, 0.0)[0:16]
        whole = bound + jnp.where(odd_y, north, south) + jnp.where(odd_z, above, below)
        fields[4, i - 3] = whole[0:16]

    loop(3, 19, own_faces)
    coarsen(1, 5)
    for pair, q in ((0, 1), (1, 3)):
        pack_coarse(cmp, pair, cm[q], cm[q + 1])
        pack_coarse(csp, pair, cs[q], cs[q + 1])
    send("coef")
    loop(1, 3, plain_faces)
    loop(19, 21, plain_faces)

    def beside(src, i):
        v = src[i]
        north, above = fy[i], fz[i]
        around = fx[i - 1] * src[i - 1] + fx[i] * src[i + 1]
        around = around + (north * next_y(v) + prev_y(north * v))
        return v, around + (above * next_z(v) + prev_z(above * v))

    def sweep(src, dst, lo, hi):
        def step(i):
            v, around = beside(src, i)
            dst[i] = (1.0 - OMEGA) * v + wt[i] * (se[i] + around)
        loop(lo, hi, step)

    receive("p")
    set_rim(pe, phalo)
    receive("s")
    set_rim(se, shalo)
    sweep(pe, p1, 1, 21)
    sweep(p1, p2, 2, 20)

    def residual(i):
        v, around = beside(p2, i)
        fields[0, i - 3] = (se[i] - dg[i] * v + around)[0:16]
    loop(3, 19, residual)
    coarsen(0, 1)
    pack_coarse(cmp, 2, cm[0, 0:64], cm[0, 64:128])
    send("rhs")

    rp = lax.broadcasted_iota(jnp.int32, (384, 64), 0)
    cp = lax.broadcasted_iota(jnp.int32, (384, 64), 1)
    place = (((rp >> 4) - (cp >> 4) == 4 + live) & ((rp & 15) == (cp & 15))).astype(f32)
    place = jnp.concatenate([place, place], axis=1).astype(jnp.bfloat16)

    def joined(part, halo, q, count):
        own = part[q].reshape(count, 8, 128)
        if q > 0:
            pair = (q - 1) // 2
            tiles = [halo[way, pair].reshape(count, 8, 128) for way in range(2)]
            rim = pair_off(*tiles, low_coarse)[(q - 1) % 2]
        elif count == 16:
            tiles = [halo[way, 2, 0:64].reshape(8, 8, 128) for way in range(2)]
            rim = jnp.concatenate(pair_off(*tiles, low_coarse), axis=0)
        else:
            tiles = [halo[way, 2].reshape(count, 8, 128) for way in range(2)]
            rim = pair_off(*tiles, low_coarse)[0]
        return jnp.concatenate([own, rim], axis=1)

    def extend(q0, q1):
        count = q1 - q0
        ahead = [joined(cr, hr, q, 4).reshape(64, 128) for q in range(q0, q1)]
        after = dot(place, jnp.concatenate(halves(jnp.concatenate(ahead, axis=1)), axis=0))
        for q in range(q0, q1):
            at = 128 * (q - q0)
            ext[q] = after[:, at:at + 128].reshape(24, 16, 128)
            ext[q, 0:5] += joined(cl, hl, q, 5)
            ext[q, 4:20] += joined(cm, hm, q, 16)

    receive("coef")
    extend(1, 5)
    zl = lax.broadcasted_iota(jnp.int32, (16, 128), 1)
    def diagonal(t):
        diag = ext[4, t] + ext[1, t] + ext[1, t - 1]
        corr[2, t] = OMEGA / jnp.where(diag > 0, diag, 1.0)
    loop(1, 23, diagonal, whole=True)
    ru = lax.broadcasted_iota(jnp.int32, (24, 256), 0)
    cu = lax.broadcasted_iota(jnp.int32, (24, 256), 1)
    same_y = (cu & 15) == jnp.where(ru < 20, ru >> 1, (ru >> 1) + 4)
    spread = jnp.concatenate(
        [(same_y & ((cu >> 4) == slots[x])).astype(f32) for x in range(width)], axis=0
    )
    er = lax.broadcasted_iota(jnp.int32, (256, 256), 0)
    ec = lax.broadcasted_iota(jnp.int32, (256, 256), 1)
    twice_z = ((ec >> 1) == (er & 127)).astype(f32).astype(jnp.bfloat16)
    receive("rhs")
    extend(0, 1)

    def first(t):
        corr[0, t] = corr[2, t] * ext[0, t]
    loop(1, 23, first, whole=True)
    for number, (lo, hi) in enumerate(((2, 22), (3, 21), (4, 20))):
        src, dst = number % 2, (number + 1) % 2
        def coarse_sweep(t):
            v = corr[src, t]
            north, above = ext[2, t], ext[3, t]
            around = ext[1, t] * corr[src, t + 1] + ext[1, t - 1] * corr[src, t - 1]
            around = around + (north * pltpu.roll(v, 15, 0) + pltpu.roll(north * v, 1, 0))
            around = around + (above * pltpu.roll(v, 127, 1) + pltpu.roll(above * v, 1, 1))
            corr[dst, t] = (1.0 - OMEGA) * v + corr[2, t] * (ext[0, t] + around)
        loop(lo, hi, coarse_sweep, whole=True)

    coarse = jnp.concatenate(halves(corr[1, 4:20].reshape(256, 128)), axis=1)
    fine = dot(dot(spread.astype(jnp.bfloat16), coarse).astype(jnp.bfloat16), twice_z)
    fine = fine.reshape(16, 24, 256)
    p1[3:19] = p2[3:19] + fine
    p1[2] = p2[2] + fine[0]
    p1[19] = p2[19] + fine[15]
    sweep(p1, rr, 3, 19)
    edge[0] = rr[3:19, 15, :]
    edge[1] = rr[3:19, 0, :]
    send("post")
    clear(rr, slice(3, 19), slice(16, 24))

    def last(i):
        v, around = beside(rr, i)
        result[i - 3] = ((1.0 - OMEGA) * v + wt[i] * (se[i] + around))[0:16]
    loop(3, 19, last)
    south = wt[3:19, 0, :] * fy[3:19, 23, :]
    north = wt[3:19, 15, :] * fy[3:19, 15, :]
    receive("post")
    result[0] += (wt[3, 0:16] * fx[2, 0:16]) * xhalo[0]
    result[15] += (wt[18, 0:16] * fx[18, 0:16]) * xhalo[1]
    result[:, 0, :] = result[:, 0, :] + south * rhalo[0]
    result[:, 15, :] = result[:, 15, :] + north * rhalo[1]
    store = pltpu.make_async_copy(result, out, local_sem.at[0])
    store.start()
    for name in kinds:
        sent(name)
    store.wait()


def body(permeability, source, pressure, aggregate):
    f32 = jnp.float32
    shape = permeability.shape
    block = pltpu.VMEM((22, 24, 256), f32)
    halo = pltpu.VMEM((2, 10, 8, 256), f32)
    hbm = pl.BlockSpec(memory_space=pltpu.HBM)
    return pl.pallas_call(
        kernel,
        out_shape=jax.ShapeDtypeStruct(shape, f32),
        in_specs=[pl.BlockSpec(memory_space=pltpu.SMEM), hbm, hbm, hbm],
        out_specs=hbm,
        scratch_shapes=[block, block, block, halo, halo, halo]
        + [block] * 8
        + [
            pltpu.VMEM((2, 16, 256), f32),
            halo,
            halo,
            halo,
            pltpu.VMEM((2, 16, 256), f32),
            pltpu.VMEM((2, 16, 256), f32),
            pltpu.VMEM((16, 16, 256), f32),
            pltpu.VMEM((5, 16, 16, 256), f32),
            pltpu.VMEM((5, 128, 128), f32),
            pltpu.VMEM((5, 40, 128), f32),
            pltpu.VMEM((5, 32, 128), f32),
            pltpu.VMEM((5, 40, 128), f32),
            pltpu.VMEM((2, 3, 128, 128), f32),
            pltpu.VMEM((2, 2, 40, 128), f32),
            pltpu.VMEM((2, 3, 128, 128), f32),
            pltpu.VMEM((2, 3, 40, 128), f32),
            pltpu.VMEM((2, 3, 32, 128), f32),
            pltpu.VMEM((5, 24, 16, 128), f32),
            pltpu.VMEM((3, 24, 16, 128), f32),
            pltpu.SemaphoreType.DMA((3,)),
            pltpu.SemaphoreType.DMA((48,)),
            pltpu.SemaphoreType.DMA((48,)),
        ],
        compiler_params=pltpu.CompilerParams(
            collective_id=0, has_side_effects=True, vmem_limit_bytes=GRANT
        ),
    )(aggregate, permeability, source, pressure)

def solution(mesh):
    spec = P(("real", "slab"), ("pencil", "sub"), None)
    return jax.shard_map(
        body, mesh=mesh, in_specs=(spec, spec, spec, P("real")), out_specs=spec, check_vma=False
    )
```

```python
import functools
import jax
import jax.numpy as jnp
from jax import lax
from jax.experimental import pallas as pl
from jax.experimental.pallas import tpu as pltpu
from jax.sharding import PartitionSpec as P

OMEGA = 0.8
GRANT = 62 * 2**20
MESH = pl.DeviceIdType.MESH

DIRS = [(dx, dy) for dx in (1, 0, -1) for dy in (1, 0, -1) if (dx, dy) != (0, 0)]
FROM = {0: 0, 1: 1, -1: 2}


def dot(a, b):
    return jnp.dot(a, b, preferred_element_type=jnp.float32)


def halves(v):
    upper = v.astype(jnp.bfloat16)
    return upper, (v - upper.astype(jnp.float32)).astype(jnp.bfloat16)


def kernel(
    agg, k_in, s_in, p_in, out,
    ke, se, pe, khalo, shalo, phalo, fx, fy, fz, dg, wt, p1, p2, rr, rhalo,
    kpack, ppack, spack, edge, xhalo, result, fields, cm, cl, cr, cs, cmp, csp, hm, hl, hr, ext, corr, local_sem, send_sem, recv_sem,
):
    f32 = jnp.float32
    width = 16
    slab, slabs = lax.axis_index("slab"), lax.axis_size("slab")
    subs = lax.axis_size("sub")
    rows = lax.axis_size("pencil") * subs
    row = lax.axis_index("pencil") * subs + lax.axis_index("sub")

    loads = [
        pltpu.make_async_copy(src, dst.at[3:19, 0:16], local_sem.at[i])
        for i, (src, dst) in enumerate(((k_in, ke), (p_in, pe), (s_in, se)))
    ]
    for load in loads:
        load.start()

    def exists(dx, dy):
        ok = None
        for pos, step, count in ((slab, dx, slabs), (row, dy, rows)):
            if step:
                here = (pos + step < count) if step > 0 else (pos > 0)
                ok = here if ok is None else jnp.logical_and(ok, here)
        return ok

    def device(dx, dy):
        r = row + dy
        return {"slab": slab + dx, "pencil": r // subs, "sub": r % subs}

    barrier = pltpu.get_barrier_semaphore()
    for dx, dy in DIRS:
        @pl.when(exists(dx, dy))
        def _():
            pl.semaphore_signal(barrier, inc=1, device_id=device(dx, dy), device_id_type=MESH)
    near_x = 1 + (slab > 0).astype(jnp.int32) + (slab < slabs - 1).astype(jnp.int32)
    near_y = 1 + (row > 0).astype(jnp.int32) + (row < rows - 1).astype(jnp.int32)

    def message(kind, d, src, dst):
        return pltpu.make_async_remote_copy(
            src_ref=src, dst_ref=dst,
            send_sem=send_sem.at[kind * 8 + d], recv_sem=recv_sem.at[kind * 8 + d],
            device_id=device(*DIRS[d]), device_id_type=MESH,
        )

    def fine_message(kind, d, body, packed, halo, wide):
        dx, dy = DIRS[d]
        if dy == 0:
            src0 = 19 - wide if dx > 0 else 3
            dst0 = 3 - wide if dx > 0 else 19
            return message(kind, d, body.at[src0:src0 + wide, 0:16], body.at[dst0:dst0 + wide, 0:16])
        src0, dst0, length = {0: (1, 1, 8), 1: (9, 0, 1), -1: (0, 9, 1)}[dx]
        return message(
            kind, d, packed.at[FROM[dy] - 1, src0:src0 + length],
            halo.at[FROM[dy] - 1, dst0:dst0 + length],
        )

    def coarse_message(kind, d, q0, q1):
        dx, dy = DIRS[d]
        if dy == 0:
            qs = pl.ds(q0, q1 - q0)
            if dx > 0:
                return message(kind, d, cs.at[qs], cl.at[qs])
            return message(kind, d, cm.at[qs, 0:32], cr.at[qs])
        here = FROM[dy] - 1
        if q0 == 0:
            if dx > 0:
                return message(kind, d, cs.at[0], hl.at[here, 2])
            if dx < 0:
                return message(kind, d, cm.at[0, 0:32], hr.at[here, 2])
            return message(kind, d, cmp.at[here, 2, 0:64], hm.at[here, 2, 0:64])
        if dx > 0:
            return message(kind, d, csp.at[here], hl.at[here, 0:2])
        if dx < 0:
            return message(kind, d, cmp.at[here, 0:2, 0:32], hr.at[here, 0:2])
        return message(kind, d, cmp.at[here, 0:2], hm.at[here, 0:2])

    def post_message(d):
        dx, dy = DIRS[d]
        if dx > 0:
            return message(5, d, rr.at[18, 0:16], xhalo.at[0])
        if dx < 0:
            return message(5, d, rr.at[3, 0:16], xhalo.at[1])
        return message(5, d, edge.at[FROM[dy] - 1], rhalo.at[FROM[dy] - 1])

    kinds = {
        "k": lambda d: fine_message(0, d, ke, kpack, khalo, 3),
        "p": lambda d: fine_message(1, d, pe, ppack, phalo, 3),
        "s": lambda d: fine_message(2, d, se, spack, shalo, 2),
        "coef": lambda d: coarse_message(3, d, 1, 5),
        "rhs": lambda d: coarse_message(4, d, 0, 1),
        "post": post_message,
    }

    def each(name):
        return [d for d in range(8) if name != "post" or 0 in DIRS[d]]

    def send(name):
        for d in each(name):
            @pl.when(exists(*DIRS[d]))
            def _():
                kinds[name](d).start()

    def receive(name):
        for d in each(name):
            dx, dy = DIRS[d]
            @pl.when(exists(-dx, -dy))
            def _():
                kinds[name](d).wait_recv()

    def sent(name):
        for d in each(name):
            @pl.when(exists(*DIRS[d]))
            def _():
                kinds[name](d).wait_send()

    low_half = lax.broadcasted_iota(jnp.int32, (1, 8, 256), 1) < 4
    low_coarse = lax.broadcasted_iota(jnp.int32, (1, 8, 128), 1) < 4

    def turned(v):
        return pltpu.roll(v, 4, 1)

    def pair_up(a, b, low):
        return jnp.where(low, turned(b), a), jnp.where(low, a, turned(b))

    def pair_off(up, down, low):
        return jnp.where(low, down, up), turned(jnp.where(low, up, down))

    def pack(body, packed):
        for at, a, b, count in ((1, 3, 11, 8), (0, 3, 4, 1), (9, 17, 18, 1)):
            for way, lo in ((0, 8), (1, 0)):
                tiles = pair_up(body[a:a + count, lo:lo + 8], body[b:b + count, lo:lo + 8], low_half)
                packed[way, at:at + count] = tiles[way]

    for name, load, parts in zip("kps", loads, ((ke, kpack), (pe, ppack), (se, spack))):
        load.wait()
        pack(*parts)
        if name == "k":
            pl.semaphore_wait(barrier, near_x * near_y - 1)
        send(name)

    def clear(ref, *index):
        view = ref.at[index]
        view[...] = jnp.zeros(view.shape, f32)

    for ref in (ke, pe):
        clear(ref, 0, slice(16, 24))
        clear(ref, 21, slice(16, 24))
    clear(rr, 2)
    clear(rr, 19)
    for dx, dy in DIRS:
        @pl.when(jnp.logical_not(exists(-dx, -dy)))
        def _():
            if dx == 0:
                clear(rhalo, FROM[dy] - 1)
            if dy == 0:
                clear(xhalo, 0 if dx > 0 else 1)
            for ref, halo, wide in ((ke, khalo, 3), (pe, phalo, 3), (se, shalo, 2)):
                if dy == 0:
                    at = slice(3 - wide, 3) if dx > 0 else slice(19, 19 + wide)
                    clear(ref, at, slice(0, 16))
                else:
                    lo, hi = {0: (1, 9), 1: (0, 1), -1: (9, 10)}[dx]
                    clear(halo, FROM[dy] - 1, slice(lo, hi))
            if dy == 0:
                clear({1: cl, -1: cr}[dx])
            else:
                clear({0: hm, 1: hl, -1: hr}[dx], FROM[dy] - 1)

    y_at = lax.broadcasted_iota(jnp.int32, (24, 256), 0)
    z_at = lax.broadcasted_iota(jnp.int32, (24, 256), 1)
    y_rel = jnp.where(y_at < 20, y_at, y_at - 24)
    y_glob = y_rel + row * width
    ends_yz = (
        (y_glob == 0).astype(f32) + (y_glob == rows * width - 1).astype(f32)
        + (z_at == 0).astype(f32) + (z_at == 255).astype(f32)
    )
    odd_y = (y_at & 1) == 1
    odd_z = (z_at & 1) == 1

    def loop(lo, hi, step):
        def run(i, carry):
            step(i)
            return carry
        lax.fori_loop(lo, hi, run, 0, unroll=True)

    def set_rim(body, halo):
        for at, a, b, count in ((1, 3, 11, 8), (0, 1, 2, 1), (9, 19, 20, 1)):
            here = slice(at, at + count)
            first, second = pair_off(halo[0, here], halo[1, here], low_half)
            body[a:a + count, 16:24] = first
            body[b:b + count, 16:24] = second

    def next_y(v):
        return pltpu.roll(v, 23, 0)

    def prev_y(v):
        return pltpu.roll(v, 1, 0)

    def next_z(v):
        return pltpu.roll(v, 255, 1)

    def prev_z(v):
        return pltpu.roll(v, 1, 1)

    def face(a, b):
        total = a + b
        return 2.0 * a * b / jnp.where(total > 0, total, 1.0)

    ids = [agg[slab * width + x] for x in range(width)]
    slots = [i - ids[0] for i in ids]
    live = slots[15]
    col = lax.broadcasted_iota(jnp.int32, (1, 256), 1)
    slot_col = jnp.zeros((1, 256), jnp.int32)
    for x in range(width):
        inside = (col >> 4) == x
        slot_col = jnp.where(inside, slots[x], slot_col)
    r168 = lax.broadcasted_iota(jnp.int32, (168, 256), 0)
    c168 = lax.broadcasted_iota(jnp.int32, (168, 256), 1)
    want = jnp.where(r168 < 128, r168 >> 3, (r168 >> 3) - 20 + live)
    gather = ((want == slot_col) & ((r168 & 7) == ((c168 & 15) >> 1))).astype(f32)
    gather = jnp.concatenate([gather, gather], axis=1).astype(jnp.bfloat16)
    zr = lax.broadcasted_iota(jnp.int32, (512, 128), 0)
    zc = lax.broadcasted_iota(jnp.int32, (512, 128), 1)
    pair_z = (((zr & 255) >> 1) == zc).astype(f32).astype(jnp.bfloat16)

    def coarsen(q0, q1):
        count = q1 - q0
        flat = fields[q0:q1].reshape(count * 256, 256)
        pairs = dot(jnp.concatenate(halves(flat), axis=1), pair_z)
        pairs = jnp.concatenate([pairs[256 * q:256 * (q + 1)] for q in range(count)], axis=1)
        sums = dot(gather, jnp.concatenate(halves(pairs), axis=0))
        for q in range(count):
            part = sums[:, 128 * q:128 * (q + 1)]
            cm[q0 + q] = part[0:128]
            cs[q0 + q] = part[128:168]

    def pack_coarse(packed, pair, a, b):
        tiles = pair_up(a.reshape(-1, 8, 128), b.reshape(-1, 8, 128), low_coarse)
        for way in range(2):
            packed[way, pair, 0:a.shape[0]] = tiles[way].reshape(a.shape)

    receive("k")
    set_rim(ke, khalo)

    def x_faces(i):
        fx[i] = face(ke[i], ke[i + 1])
    loop(0, 21, x_faces)

    def other_faces(i):
        k = ke[i]
        north = face(k, next_y(k))
        above = jnp.where(z_at == 255, 0.0, face(k, next_z(k)))
        south, below = prev_y(north), prev_z(above)
        x_glob = slab * width + i - 3
        ends_x = (x_glob == 0).astype(f32) + (x_glob == slabs * width - 1).astype(f32)
        bound = 2.0 * k * (ends_yz + ends_x)
        fy[i] = north
        fz[i] = above
        diag = fx[i - 1] + fx[i] + north + south + above + below + bound
        dg[i] = diag
        wt[i] = OMEGA / jnp.where(diag > 0, diag, 1.0)
        return north, above, south, below, bound

    def plain_faces(i):
        other_faces(i)

    def own_faces(i):
        north, above, south, below, bound = other_faces(i)
        x = slab * width + i - 3
        crossing = agg[x] != agg[jnp.minimum(x + 1, slabs * width - 1)]
        fields[1, i - 3] = fx[i, 0:16] * crossing.astype(f32)
        fields[2, i - 3] = jnp.where(odd_y, north, 0.0)[0:16]
        fields[3, i - 3] = jnp.where(odd_z, above, 0.0)[0:16]
        whole = bound + jnp.where(odd_y, north, south) + jnp.where(odd_z, above, below)
        fields[4, i - 3] = whole[0:16]

    loop(3, 19, own_faces)
    coarsen(1, 5)
    for pair, q in ((0, 1), (1, 3)):
        pack_coarse(cmp, pair, cm[q], cm[q + 1])
        pack_coarse(csp, pair, cs[q], cs[q + 1])
    send("coef")
    loop(1, 3, plain_faces)
    loop(19, 21, plain_faces)

    def beside(src, i):
        v = src[i]
        north, above = fy[i], fz[i]
        around = fx[i - 1] * src[i - 1] + fx[i] * src[i + 1]
        around = around + (north * next_y(v) + prev_y(north * v))
        return v, around + (above * next_z(v) + prev_z(above * v))

    def sweep(src, dst, lo, hi):
        def step(i):
            v, around = beside(src, i)
            dst[i] = (1.0 - OMEGA) * v + wt[i] * (se[i] + around)
        loop(lo, hi, step)

    receive("p")
    set_rim(pe, phalo)
    receive("s")
    set_rim(se, shalo)
    sweep(pe, p1, 1, 21)
    sweep(p1, p2, 2, 20)

    def residual(i):
        v, around = beside(p2, i)
        fields[0, i - 3] = (se[i] - dg[i] * v + around)[0:16]
    loop(3, 19, residual)
    coarsen(0, 1)
    pack_coarse(cmp, 2, cm[0, 0:64], cm[0, 64:128])
    send("rhs")

    rp = lax.broadcasted_iota(jnp.int32, (384, 64), 0)
    cp = lax.broadcasted_iota(jnp.int32, (384, 64), 1)
    place = (((rp >> 4) - (cp >> 4) == 4 + live) & ((rp & 15) == (cp & 15))).astype(f32)
    place = jnp.concatenate([place, place], axis=1).astype(jnp.bfloat16)

    def joined(part, halo, q, count):
        own = part[q].reshape(count, 8, 128)
        if q > 0:
            pair = (q - 1) // 2
            tiles = [halo[way, pair].reshape(count, 8, 128) for way in range(2)]
            rim = pair_off(*tiles, low_coarse)[(q - 1) % 2]
        elif count == 16:
            tiles = [halo[way, 2, 0:64].reshape(8, 8, 128) for way in range(2)]
            rim = jnp.concatenate(pair_off(*tiles, low_coarse), axis=0)
        else:
            tiles = [halo[way, 2].reshape(count, 8, 128) for way in range(2)]
            rim = pair_off(*tiles, low_coarse)[0]
        return jnp.concatenate([own, rim], axis=1)

    def extend(q0, q1):
        count = q1 - q0
        ahead = [joined(cr, hr, q, 4).reshape(64, 128) for q in range(q0, q1)]
        after = dot(place, jnp.concatenate(halves(jnp.concatenate(ahead, axis=1)), axis=0))
        for q in range(q0, q1):
            at = 128 * (q - q0)
            ext[q] = after[:, at:at + 128].reshape(24, 16, 128)
            ext[q, 0:5] += joined(cl, hl, q, 5)
            ext[q, 4:20] += joined(cm, hm, q, 16)

    receive("coef")
    extend(1, 5)
    zl = lax.broadcasted_iota(jnp.int32, (16, 128), 1)
    def diagonal(t):
        diag = ext[4, t] + ext[1, t] + ext[1, t - 1]
        corr[2, t] = OMEGA / jnp.where(diag > 0, diag, 1.0)
    loop(1, 23, diagonal)
    ru = lax.broadcasted_iota(jnp.int32, (24, 256), 0)
    cu = lax.broadcasted_iota(jnp.int32, (24, 256), 1)
    same_y = (cu & 15) == jnp.where(ru < 20, ru >> 1, (ru >> 1) + 4)
    spread = jnp.concatenate(
        [(same_y & ((cu >> 4) == slots[x])).astype(f32) for x in range(width)], axis=0
    )
    er = lax.broadcasted_iota(jnp.int32, (256, 256), 0)
    ec = lax.broadcasted_iota(jnp.int32, (256, 256), 1)
    twice_z = ((ec >> 1) == (er & 127)).astype(f32).astype(jnp.bfloat16)
    receive("rhs")
    extend(0, 1)

    def first(t):
        corr[0, t] = corr[2, t] * ext[0, t]
    loop(1, 23, first)
    for number, (lo, hi) in enumerate(((2, 22), (3, 21), (4, 20))):
        src, dst = number % 2, (number + 1) % 2
        def coarse_sweep(t):
            v = corr[src, t]
            north, above = ext[2, t], ext[3, t]
            around = ext[1, t] * corr[src, t + 1] + ext[1, t - 1] * corr[src, t - 1]
            around = around + (north * pltpu.roll(v, 15, 0) + pltpu.roll(north * v, 1, 0))
            around = around + (above * pltpu.roll(v, 127, 1) + pltpu.roll(above * v, 1, 1))
            corr[dst, t] = (1.0 - OMEGA) * v + corr[2, t] * (ext[0, t] + around)
        loop(lo, hi, coarse_sweep)

    coarse = jnp.concatenate(halves(corr[1, 4:20].reshape(256, 128)), axis=1)
    fine = dot(dot(spread.astype(jnp.bfloat16), coarse).astype(jnp.bfloat16), twice_z)
    fine = fine.reshape(16, 24, 256)
    p1[3:19] = p2[3:19] + fine
    p1[2] = p2[2] + fine[0]
    p1[19] = p2[19] + fine[15]
    sweep(p1, rr, 3, 19)
    edge[0] = rr[3:19, 15, :]
    edge[1] = rr[3:19, 0, :]
    send("post")
    clear(rr, slice(3, 19), slice(16, 24))

    def last(i):
        v, around = beside(rr, i)
        result[i - 3] = ((1.0 - OMEGA) * v + wt[i] * (se[i] + around))[0:16]
    loop(3, 19, last)
    south = wt[3:19, 0, :] * fy[3:19, 23, :]
    north = wt[3:19, 15, :] * fy[3:19, 15, :]
    receive("post")
    result[0] += (wt[3, 0:16] * fx[2, 0:16]) * xhalo[0]
    result[15] += (wt[18, 0:16] * fx[18, 0:16]) * xhalo[1]
    result[:, 0, :] = result[:, 0, :] + south * rhalo[0]
    result[:, 15, :] = result[:, 15, :] + north * rhalo[1]
    store = pltpu.make_async_copy(result, out, local_sem.at[0])
    store.start()
    for name in kinds:
        sent(name)
    store.wait()


def body(permeability, source, pressure, aggregate):
    f32 = jnp.float32
    shape = permeability.shape
    block = pltpu.VMEM((22, 24, 256), f32)
    halo = pltpu.VMEM((2, 10, 8, 256), f32)
    hbm = pl.BlockSpec(memory_space=pltpu.HBM)
    return pl.pallas_call(
        kernel,
        out_shape=jax.ShapeDtypeStruct(shape, f32),
        in_specs=[pl.BlockSpec(memory_space=pltpu.SMEM), hbm, hbm, hbm],
        out_specs=hbm,
        scratch_shapes=[block, block, block, halo, halo, halo]
        + [block] * 8
        + [
            pltpu.VMEM((2, 16, 256), f32),
            halo,
            halo,
            halo,
            pltpu.VMEM((2, 16, 256), f32),
            pltpu.VMEM((2, 16, 256), f32),
            pltpu.VMEM((16, 16, 256), f32),
            pltpu.VMEM((5, 16, 16, 256), f32),
            pltpu.VMEM((5, 128, 128), f32),
            pltpu.VMEM((5, 40, 128), f32),
            pltpu.VMEM((5, 32, 128), f32),
            pltpu.VMEM((5, 40, 128), f32),
            pltpu.VMEM((2, 3, 128, 128), f32),
            pltpu.VMEM((2, 2, 40, 128), f32),
            pltpu.VMEM((2, 3, 128, 128), f32),
            pltpu.VMEM((2, 3, 40, 128), f32),
            pltpu.VMEM((2, 3, 32, 128), f32),
            pltpu.VMEM((5, 24, 16, 128), f32),
            pltpu.VMEM((3, 24, 16, 128), f32),
            pltpu.SemaphoreType.DMA((3,)),
            pltpu.SemaphoreType.DMA((48,)),
            pltpu.SemaphoreType.DMA((48,)),
        ],
        compiler_params=pltpu.CompilerParams(
            collective_id=0, has_side_effects=True, vmem_limit_bytes=GRANT
        ),
    )(aggregate, permeability, source, pressure)

def solution(mesh):
    spec = P(("real", "slab"), ("pencil", "sub"), None)
    return jax.shard_map(
        body, mesh=mesh, in_specs=(spec, spec, spec, P("real")), out_specs=spec, check_vma=False
    )
```

```python
import functools
import jax
import jax.numpy as jnp
from jax import lax
from jax.experimental import pallas as pl
from jax.experimental.pallas import tpu as pltpu
from jax.sharding import PartitionSpec as P

OMEGA = 0.8
GRANT = 62 * 2**20
MESH = pl.DeviceIdType.MESH

DIRS = [(dx, dy) for dx in (1, 0, -1) for dy in (1, 0, -1) if (dx, dy) != (0, 0)]
FROM = {0: 0, 1: 1, -1: 2}


def dot(a, b):
    return jnp.dot(a, b, preferred_element_type=jnp.float32)


def halves(v):
    upper = v.astype(jnp.bfloat16)
    return upper, (v - upper.astype(jnp.float32)).astype(jnp.bfloat16)


def kernel(
    agg, k_in, s_in, p_in, out,
    ke, se, pe, khalo, shalo, phalo, fx, fy, fz, dg, wt, p1, p2, rr, rhalo,
    kpack, ppack, spack, edge, xhalo, result, fields, cm, cl, cr, cs, cmp, csp, hm, hl, hr, ext, corr, local_sem, send_sem, recv_sem,
):
    f32 = jnp.float32
    width = 16
    slab, slabs = lax.axis_index("slab"), lax.axis_size("slab")
    subs = lax.axis_size("sub")
    rows = lax.axis_size("pencil") * subs
    row = lax.axis_index("pencil") * subs + lax.axis_index("sub")

    loads = [
        pltpu.make_async_copy(src, dst.at[3:19, 0:16], local_sem.at[i])
        for i, (src, dst) in enumerate(((k_in, ke), (p_in, pe), (s_in, se)))
    ]
    for load in loads:
        load.start()

    def exists(dx, dy):
        ok = None
        for pos, step, count in ((slab, dx, slabs), (row, dy, rows)):
            if step:
                here = (pos + step < count) if step > 0 else (pos > 0)
                ok = here if ok is None else jnp.logical_and(ok, here)
        return ok

    def device(dx, dy):
        r = row + dy
        return {"slab": slab + dx, "pencil": r // subs, "sub": r % subs}

    barrier = pltpu.get_barrier_semaphore()
    for dx, dy in DIRS:
        @pl.when(exists(dx, dy))
        def _():
            pl.semaphore_signal(barrier, inc=1, device_id=device(dx, dy), device_id_type=MESH)
    near_x = 1 + (slab > 0).astype(jnp.int32) + (slab < slabs - 1).astype(jnp.int32)
    near_y = 1 + (row > 0).astype(jnp.int32) + (row < rows - 1).astype(jnp.int32)

    def message(kind, d, src, dst):
        return pltpu.make_async_remote_copy(
            src_ref=src, dst_ref=dst,
            send_sem=send_sem.at[kind * 8 + d], recv_sem=recv_sem.at[kind * 8 + d],
            device_id=device(*DIRS[d]), device_id_type=MESH,
        )

    def fine_message(kind, d, body, packed, halo, wide):
        dx, dy = DIRS[d]
        if dy == 0:
            src0 = 19 - wide if dx > 0 else 3
            dst0 = 3 - wide if dx > 0 else 19
            return message(kind, d, body.at[src0:src0 + wide, 0:16], body.at[dst0:dst0 + wide, 0:16])
        src0, dst0, length = {0: (1, 1, 8), 1: (9, 0, 1), -1: (0, 9, 1)}[dx]
        return message(
            kind, d, packed.at[FROM[dy] - 1, src0:src0 + length],
            halo.at[FROM[dy] - 1, dst0:dst0 + length],
        )

    def coarse_message(kind, d, q0, q1):
        dx, dy = DIRS[d]
        if dy == 0:
            qs = pl.ds(q0, q1 - q0)
            if dx > 0:
                return message(kind, d, cs.at[qs], cl.at[qs])
            return message(kind, d, cm.at[qs, 0:32], cr.at[qs])
        here = FROM[dy] - 1
        if q0 == 0:
            if dx > 0:
                return message(kind, d, cs.at[0], hl.at[here, 2])
            if dx < 0:
                return message(kind, d, cm.at[0, 0:32], hr.at[here, 2])
            return message(kind, d, cmp.at[here, 2, 0:64], hm.at[here, 2, 0:64])
        if dx > 0:
            return message(kind, d, csp.at[here], hl.at[here, 0:2])
        if dx < 0:
            return message(kind, d, cmp.at[here, 0:2, 0:32], hr.at[here, 0:2])
        return message(kind, d, cmp.at[here, 0:2], hm.at[here, 0:2])

    def post_message(d):
        dx, dy = DIRS[d]
        if dx > 0:
            return message(5, d, rr.at[18, 0:16], xhalo.at[0])
        if dx < 0:
            return message(5, d, rr.at[3, 0:16], xhalo.at[1])
        return message(5, d, edge.at[FROM[dy] - 1], rhalo.at[FROM[dy] - 1])

    kinds = {
        "k": lambda d: fine_message(0, d, ke, kpack, khalo, 3),
        "p": lambda d: fine_message(1, d, pe, ppack, phalo, 3),
        "s": lambda d: fine_message(2, d, se, spack, shalo, 2),
        "coef": lambda d: coarse_message(3, d, 1, 5),
        "rhs": lambda d: coarse_message(4, d, 0, 1),
        "post": post_message,
    }

    def each(name):
        return [d for d in range(8) if name != "post" or 0 in DIRS[d]]

    def send(name):
        for d in each(name):
            @pl.when(exists(*DIRS[d]))
            def _():
                kinds[name](d).start()

    def receive(name):
        for d in each(name):
            dx, dy = DIRS[d]
            @pl.when(exists(-dx, -dy))
            def _():
                kinds[name](d).wait_recv()

    def sent(name):
        for d in each(name):
            @pl.when(exists(*DIRS[d]))
            def _():
                kinds[name](d).wait_send()

    low_half = lax.broadcasted_iota(jnp.int32, (1, 8, 256), 1) < 4
    low_coarse = lax.broadcasted_iota(jnp.int32, (1, 8, 128), 1) < 4

    def turned(v):
        return pltpu.roll(v, 4, 1)

    def pair_up(a, b, low):
        return jnp.where(low, turned(b), a), jnp.where(low, a, turned(b))

    def pair_off(up, down, low):
        return jnp.where(low, down, up), turned(jnp.where(low, up, down))

    def pack(body, packed):
        for at, a, b, count in ((1, 3, 11, 8), (0, 3, 4, 1), (9, 17, 18, 1)):
            for way, lo in ((0, 8), (1, 0)):
                tiles = pair_up(body[a:a + count, lo:lo + 8], body[b:b + count, lo:lo + 8], low_half)
                packed[way, at:at + count] = tiles[way]

    for name, load, parts in zip("kps", loads, ((ke, kpack), (pe, ppack), (se, spack))):
        load.wait()
        pack(*parts)
        if name == "k":
            pl.semaphore_wait(barrier, near_x * near_y - 1)
        send(name)

    def clear(ref, *index):
        view = ref.at[index]
        view[...] = jnp.zeros(view.shape, f32)

    for ref in (ke, pe):
        clear(ref, 0, slice(16, 24))
        clear(ref, 21, slice(16, 24))
    clear(rr, 2)
    clear(rr, 19)
    for dx, dy in DIRS:
        @pl.when(jnp.logical_not(exists(-dx, -dy)))
        def _():
            if dx == 0:
                clear(rhalo, FROM[dy] - 1)
            if dy == 0:
                clear(xhalo, 0 if dx > 0 else 1)
            for ref, halo, wide in ((ke, khalo, 3), (pe, phalo, 3), (se, shalo, 2)):
                if dy == 0:
                    at = slice(3 - wide, 3) if dx > 0 else slice(19, 19 + wide)
                    clear(ref, at, slice(0, 16))
                else:
                    lo, hi = {0: (1, 9), 1: (0, 1), -1: (9, 10)}[dx]
                    clear(halo, FROM[dy] - 1, slice(lo, hi))
            if dy == 0:
                clear({1: cl, -1: cr}[dx])
            else:
                clear({0: hm, 1: hl, -1: hr}[dx], FROM[dy] - 1)

    y_at = lax.broadcasted_iota(jnp.int32, (24, 256), 0)
    z_at = lax.broadcasted_iota(jnp.int32, (24, 256), 1)
    y_rel = jnp.where(y_at < 20, y_at, y_at - 24)
    y_glob = y_rel + row * width
    ends_yz = (
        (y_glob == 0).astype(f32) + (y_glob == rows * width - 1).astype(f32)
        + (z_at == 0).astype(f32) + (z_at == 255).astype(f32)
    )
    odd_y = (y_at & 1) == 1
    odd_z = (z_at & 1) == 1

    def loop(lo, hi, step):
        def run(i, carry):
            step(i)
            return carry
        lax.fori_loop(lo, hi, run, 0, unroll=True)

    def set_rim(body, halo):
        for at, a, b, count in ((1, 3, 11, 8), (0, 1, 2, 1), (9, 19, 20, 1)):
            here = slice(at, at + count)
            first, second = pair_off(halo[0, here], halo[1, here], low_half)
            body[a:a + count, 16:24] = first
            body[b:b + count, 16:24] = second

    def next_y(v):
        return pltpu.roll(v, 23, 0)

    def prev_y(v):
        return pltpu.roll(v, 1, 0)

    def next_z(v):
        return pltpu.roll(v, 255, 1)

    def prev_z(v):
        return pltpu.roll(v, 1, 1)

    def face(a, b):
        total = a + b
        return 2.0 * a * b / jnp.where(total > 0, total, 1.0)

    ids = [agg[slab * width + x] for x in range(width)]
    slots = [i - ids[0] for i in ids]
    live = slots[15]
    col = lax.broadcasted_iota(jnp.int32, (1, 256), 1)
    slot_col = jnp.zeros((1, 256), jnp.int32)
    for x in range(width):
        inside = (col >> 4) == x
        slot_col = jnp.where(inside, slots[x], slot_col)
    r168 = lax.broadcasted_iota(jnp.int32, (168, 256), 0)
    c168 = lax.broadcasted_iota(jnp.int32, (168, 256), 1)
    want = jnp.where(r168 < 128, r168 >> 3, (r168 >> 3) - 20 + live)
    gather = ((want == slot_col) & ((r168 & 7) == ((c168 & 15) >> 1))).astype(f32)
    gather = jnp.concatenate([gather, gather], axis=1).astype(jnp.bfloat16)
    zr = lax.broadcasted_iota(jnp.int32, (512, 128), 0)
    zc = lax.broadcasted_iota(jnp.int32, (512, 128), 1)
    pair_z = (((zr & 255) >> 1) == zc).astype(f32).astype(jnp.bfloat16)

    def coarsen(q0, q1):
        count = q1 - q0
        flat = fields[q0:q1].reshape(count * 256, 256)
        pairs = dot(jnp.concatenate(halves(flat), axis=1), pair_z)
        pairs = jnp.concatenate([pairs[256 * q:256 * (q + 1)] for q in range(count)], axis=1)
        sums = dot(gather, jnp.concatenate(halves(pairs), axis=0))
        for q in range(count):
            part = sums[:, 128 * q:128 * (q + 1)]
            cm[q0 + q] = part[0:128]
            cs[q0 + q] = part[128:168]

    def pack_coarse(packed, pair, a, b):
        tiles = pair_up(a.reshape(-1, 8, 128), b.reshape(-1, 8, 128), low_coarse)
        for way in range(2):
            packed[way, pair, 0:a.shape[0]] = tiles[way].reshape(a.shape)

    own, rim, every = slice(0, 16), slice(16, 24), slice(0, 24)

    def x_faces(part):
        def step(i):
            fx[i, part] = face(ke[i, part], ke[i + 1, part])
        return step

    def z_faces(part):
        def step(i):
            k = ke[i, part]
            fz[i, part] = jnp.where(z_at[part] == 255, 0.0, face(k, next_z(k)))
        return step

    loop(3, 18, x_faces(own))
    loop(3, 19, z_faces(own))
    receive("k")
    set_rim(ke, khalo)
    loop(3, 18, x_faces(rim))
    loop(3, 19, z_faces(rim))
    for lo, hi in ((0, 3), (18, 21)):
        loop(lo, hi, x_faces(every))
    for lo, hi in ((1, 3), (19, 21)):
        loop(lo, hi, z_faces(every))

    def other_faces(i):
        k = ke[i]
        north = face(k, next_y(k))
        above = fz[i]
        south, below = prev_y(north), prev_z(above)
        x_glob = slab * width + i - 3
        ends_x = (x_glob == 0).astype(f32) + (x_glob == slabs * width - 1).astype(f32)
        bound = 2.0 * k * (ends_yz + ends_x)
        fy[i] = north
        diag = fx[i - 1] + fx[i] + north + south + above + below + bound
        dg[i] = diag
        wt[i] = OMEGA / jnp.where(diag > 0, diag, 1.0)
        return north, above, south, below, bound

    def plain_faces(i):
        other_faces(i)

    def own_faces(i):
        north, above, south, below, bound = other_faces(i)
        x = slab * width + i - 3
        crossing = agg[x] != agg[jnp.minimum(x + 1, slabs * width - 1)]
        fields[1, i - 3] = fx[i, 0:16] * crossing.astype(f32)
        fields[2, i - 3] = jnp.where(odd_y, north, 0.0)[0:16]
        fields[3, i - 3] = jnp.where(odd_z, above, 0.0)[0:16]
        whole = bound + jnp.where(odd_y, north, south) + jnp.where(odd_z, above, below)
        fields[4, i - 3] = whole[0:16]

    loop(3, 19, own_faces)
    coarsen(1, 5)
    for pair, q in ((0, 1), (1, 3)):
        pack_coarse(cmp, pair, cm[q], cm[q + 1])
        pack_coarse(csp, pair, cs[q], cs[q + 1])
    send("coef")
    loop(1, 3, plain_faces)
    loop(19, 21, plain_faces)

    def beside(src, i):
        v = src[i]
        north, above = fy[i], fz[i]
        around = fx[i - 1] * src[i - 1] + fx[i] * src[i + 1]
        around = around + (north * next_y(v) + prev_y(north * v))
        return v, around + (above * next_z(v) + prev_z(above * v))

    def sweep(src, dst, lo, hi):
        def step(i):
            v, around = beside(src, i)
            dst[i] = (1.0 - OMEGA) * v + wt[i] * (se[i] + around)
        loop(lo, hi, step)

    receive("p")
    set_rim(pe, phalo)
    receive("s")
    set_rim(se, shalo)
    sweep(pe, p1, 1, 21)
    sweep(p1, p2, 2, 20)

    def residual(i):
        v, around = beside(p2, i)
        fields[0, i - 3] = (se[i] - dg[i] * v + around)[0:16]
    loop(3, 19, residual)
    coarsen(0, 1)
    pack_coarse(cmp, 2, cm[0, 0:64], cm[0, 64:128])
    send("rhs")

    rp = lax.broadcasted_iota(jnp.int32, (384, 64), 0)
    cp = lax.broadcasted_iota(jnp.int32, (384, 64), 1)
    place = (((rp >> 4) - (cp >> 4) == 4 + live) & ((rp & 15) == (cp & 15))).astype(f32)
    place = jnp.concatenate([place, place], axis=1).astype(jnp.bfloat16)

    def joined(part, halo, q, count):
        own = part[q].reshape(count, 8, 128)
        if q > 0:
            pair = (q - 1) // 2
            tiles = [halo[way, pair].reshape(count, 8, 128) for way in range(2)]
            rim = pair_off(*tiles, low_coarse)[(q - 1) % 2]
        elif count == 16:
            tiles = [halo[way, 2, 0:64].reshape(8, 8, 128) for way in range(2)]
            rim = jnp.concatenate(pair_off(*tiles, low_coarse), axis=0)
        else:
            tiles = [halo[way, 2].reshape(count, 8, 128) for way in range(2)]
            rim = pair_off(*tiles, low_coarse)[0]
        return jnp.concatenate([own, rim], axis=1)

    def extend(q0, q1):
        count = q1 - q0
        ahead = [joined(cr, hr, q, 4).reshape(64, 128) for q in range(q0, q1)]
        after = dot(place, jnp.concatenate(halves(jnp.concatenate(ahead, axis=1)), axis=0))
        for q in range(q0, q1):
            at = 128 * (q - q0)
            ext[q] = after[:, at:at + 128].reshape(24, 16, 128)
            ext[q, 0:5] += joined(cl, hl, q, 5)
            ext[q, 4:20] += joined(cm, hm, q, 16)

    receive("coef")
    extend(1, 5)
    zl = lax.broadcasted_iota(jnp.int32, (16, 128), 1)
    def diagonal(t):
        diag = ext[4, t] + ext[1, t] + ext[1, t - 1]
        corr[2, t] = OMEGA / jnp.where(diag > 0, diag, 1.0)
    loop(1, 23, diagonal)
    ru = lax.broadcasted_iota(jnp.int32, (24, 256), 0)
    cu = lax.broadcasted_iota(jnp.int32, (24, 256), 1)
    same_y = (cu & 15) == jnp.where(ru < 20, ru >> 1, (ru >> 1) + 4)
    spread = jnp.concatenate(
        [(same_y & ((cu >> 4) == slots[x])).astype(f32) for x in range(width)], axis=0
    )
    er = lax.broadcasted_iota(jnp.int32, (256, 256), 0)
    ec = lax.broadcasted_iota(jnp.int32, (256, 256), 1)
    twice_z = ((ec >> 1) == (er & 127)).astype(f32).astype(jnp.bfloat16)
    receive("rhs")
    extend(0, 1)

    def first(t):
        corr[0, t] = corr[2, t] * ext[0, t]
    loop(1, 23, first)
    for number, (lo, hi) in enumerate(((2, 22), (3, 21), (4, 20))):
        src, dst = number % 2, (number + 1) % 2
        def coarse_sweep(t):
            v = corr[src, t]
            north, above = ext[2, t], ext[3, t]
            around = ext[1, t] * corr[src, t + 1] + ext[1, t - 1] * corr[src, t - 1]
            around = around + (north * pltpu.roll(v, 15, 0) + pltpu.roll(north * v, 1, 0))
            around = around + (above * pltpu.roll(v, 127, 1) + pltpu.roll(above * v, 1, 1))
            corr[dst, t] = (1.0 - OMEGA) * v + corr[2, t] * (ext[0, t] + around)
        loop(lo, hi, coarse_sweep)

    coarse = jnp.concatenate(halves(corr[1, 4:20].reshape(256, 128)), axis=1)
    fine = dot(dot(spread.astype(jnp.bfloat16), coarse).astype(jnp.bfloat16), twice_z)
    fine = fine.reshape(16, 24, 256)
    p1[3:19] = p2[3:19] + fine
    p1[2] = p2[2] + fine[0]
    p1[19] = p2[19] + fine[15]
    sweep(p1, rr, 3, 19)
    edge[0] = rr[3:19, 15, :]
    edge[1] = rr[3:19, 0, :]
    send("post")
    clear(rr, slice(3, 19), slice(16, 24))

    def last(i):
        v, around = beside(rr, i)
        result[i - 3] = ((1.0 - OMEGA) * v + wt[i] * (se[i] + around))[0:16]
    loop(3, 19, last)
    south = wt[3:19, 0, :] * fy[3:19, 23, :]
    north = wt[3:19, 15, :] * fy[3:19, 15, :]
    receive("post")
    result[0] += (wt[3, 0:16] * fx[2, 0:16]) * xhalo[0]
    result[15] += (wt[18, 0:16] * fx[18, 0:16]) * xhalo[1]
    result[:, 0, :] = result[:, 0, :] + south * rhalo[0]
    result[:, 15, :] = result[:, 15, :] + north * rhalo[1]
    store = pltpu.make_async_copy(result, out, local_sem.at[0])
    store.start()
    for name in kinds:
        sent(name)
    store.wait()


def body(permeability, source, pressure, aggregate):
    f32 = jnp.float32
    shape = permeability.shape
    block = pltpu.VMEM((22, 24, 256), f32)
    halo = pltpu.VMEM((2, 10, 8, 256), f32)
    hbm = pl.BlockSpec(memory_space=pltpu.HBM)
    return pl.pallas_call(
        kernel,
        out_shape=jax.ShapeDtypeStruct(shape, f32),
        in_specs=[pl.BlockSpec(memory_space=pltpu.SMEM), hbm, hbm, hbm],
        out_specs=hbm,
        scratch_shapes=[block, block, block, halo, halo, halo]
        + [block] * 8
        + [
            pltpu.VMEM((2, 16, 256), f32),
            halo,
            halo,
            halo,
            pltpu.VMEM((2, 16, 256), f32),
            pltpu.VMEM((2, 16, 256), f32),
            pltpu.VMEM((16, 16, 256), f32),
            pltpu.VMEM((5, 16, 16, 256), f32),
            pltpu.VMEM((5, 128, 128), f32),
            pltpu.VMEM((5, 40, 128), f32),
            pltpu.VMEM((5, 32, 128), f32),
            pltpu.VMEM((5, 40, 128), f32),
            pltpu.VMEM((2, 3, 128, 128), f32),
            pltpu.VMEM((2, 2, 40, 128), f32),
            pltpu.VMEM((2, 3, 128, 128), f32),
            pltpu.VMEM((2, 3, 40, 128), f32),
            pltpu.VMEM((2, 3, 32, 128), f32),
            pltpu.VMEM((5, 24, 16, 128), f32),
            pltpu.VMEM((3, 24, 16, 128), f32),
            pltpu.SemaphoreType.DMA((3,)),
            pltpu.SemaphoreType.DMA((48,)),
            pltpu.SemaphoreType.DMA((48,)),
        ],
        compiler_params=pltpu.CompilerParams(
            collective_id=0, has_side_effects=True, vmem_limit_bytes=GRANT
        ),
    )(aggregate, permeability, source, pressure)

def solution(mesh):
    spec = P(("real", "slab"), ("pencil", "sub"), None)
    return jax.shard_map(
        body, mesh=mesh, in_specs=(spec, spec, spec, P("real")), out_specs=spec, check_vma=False
    )
```
